256 devices in a mesh: dp: 32 (over z, x_lo, core), fsdp: 8 (over x_hi, y).
Axes of the slice: x: 4 (x_hi: 2, x_lo: 2; x = x_hi * 2 + x_lo), y: 4, z: 8, core: 2. Of those that a mesh axis runs over, the one named last changes fastest.
Arguments:
- grads: bfloat16 [32, 2, 8192, 1024], P('dp', None, 'fsdp'), may hold values from -1.1953125 to 1.1953125
- raw_proj: float32 [2, 1024, 512], P(None, 'fsdp'), may hold values from -6 to 6
- bucket_owner: int32 [2, 512], P(None, 'fsdp'), may hold values from 0 to 31, as said below
- first_moment: float32 [2, 8, 128, 16, 512], P(None, 'fsdp', 'dp'), may hold values from -0.6 to 0.6
- second_moment: float32 [2, 8, 128, 16, 512], P(None, 'fsdp', 'dp'), may hold values from 0.01 to 0.05
Outputs:
- weight_delta: bfloat16 [2, 8192, 1024], P(None, 'fsdp')
- first_out: float32 [2, 8, 128, 16, 512], P(None, 'fsdp', 'dp')
- second_out: float32 [2, 8, 128, 16, 512], P(None, 'fsdp', 'dp')
The draws below stay inside these ranges and needn't reach their ends.
Inputs may be any that keep to these rules, and one draw needn't show every extreme that they name: `bucket_owner`: within each matrix and each block of 64 buckets of one fsdp index, no owner holds more than 4 buckets, and one owner holds exactly 4.
All inputs are finite; a program needn't handle non-finite values.
Results may differ from the reference program's by a relative error of at most 0.0062.
Values may be sent and summed in bfloat16 or wider, within the bound.
A program may use at most 64 MiB of HBM per device.

```python
import math
import jax
import jax.numpy as jnp
from jax import lax

D = 8192
KV = 1024
R = 512
MATS = 2
BROWS = 16
NB = 64
CAP = 4
SLOTS = 128
N_DP = 32
N_FSDP = 8


def owners_of_block(key):
    key_full, key_scores, key_order = jax.random.split(key, 3)
    owner_count = SLOTS // CAP
    full_owner = jax.random.randint(key_full, (), 0, owner_count)
    scores = jax.random.permutation(key_scores, SLOTS).astype(jnp.int32)
    slot_ids = jnp.arange(SLOTS, dtype=jnp.int32)
    slot_owner = slot_ids // CAP
    scores = jnp.where(slot_owner == full_owner, slot_ids % CAP - CAP, scores)
    ordered = jnp.argsort(scores, stable=True)
    chosen = ordered[:NB] // CAP
    shuffle = jax.random.permutation(key_order, NB)
    return chosen[shuffle].astype(jnp.int32)


def draw_bucket_owner(key, part):
    blocks = D // BROWS // NB
    keys = jax.random.split(jax.random.fold_in(key, 17), MATS * blocks)
    table = jax.vmap(owners_of_block)(keys)
    return table.reshape(MATS, blocks * NB).astype(jnp.int32)


def level_of(stream_key, dims, pieces, smallest, high):
    factor_of = 1.0
    for position, shards_of in pieces:
        steps = jax.random.uniform(jax.random.fold_in(jax.random.fold_in(stream_key, 6), position), (shards_of,), jnp.float32, smallest / len(pieces), high / len(pieces))
        factor_of = factor_of * jnp.repeat(jnp.exp(steps), dims[position] // shards_of).reshape((-1,) + (1,) * (len(dims) - 1 - position))
    return factor_of


def scatter_about(own_key, dims, deviation, limit, pieces=(), kind=jnp.bfloat16):
    entries = jax.random.normal(own_key, dims, jnp.float32) * deviation
    if len(pieces) > 0:
        entries = level_of(own_key, dims, pieces, -0.22, 0.18) * entries
    return jnp.clip(entries, min=-limit, max=limit).astype(kind)


def setup_inputs(seed: int = 0) -> dict:
    seeds = jax.random.split(jax.random.key(seed), 6)
    return {
        "grads": scatter_about(seeds[0], (N_DP, MATS, D, KV), 0.2, 1.1953125, ((0, 32), (2, 8))),
        "raw_proj": scatter_about(seeds[1], (MATS, KV, R), 1.0, 6.0, ((1, 8),), jnp.float32),
        "bucket_owner": draw_bucket_owner(jax.random.fold_in(seeds[5], 71), 0),
        "first_moment": scatter_about(seeds[3], (MATS, N_FSDP, SLOTS, BROWS, R), 0.1, 0.6, ((1, 8), (2, 32)), jnp.float32),
        "second_moment": jnp.clip(jnp.exp(math.log(0.05) - 1.609438 * jax.random.uniform(seeds[4], (MATS, N_FSDP, SLOTS, BROWS, R), jnp.float32) ** level_of(seeds[4], (MATS, N_FSDP, SLOTS, BROWS, R), ((1, 8), (2, 32)), -0.2, 0.2)), 0.01, 0.05),
    }


def cholesky_basis(raw_rows):
    gram = jnp.einsum('mkr,mks->mrs', raw_rows, raw_rows, precision=lax.Precision.HIGHEST)
    factor = jnp.linalg.cholesky(gram)
    basis = lax.linalg.triangular_solve(factor, raw_rows, left_side=False, lower=True, transpose_a=True)
    return basis.astype(jnp.bfloat16)

def bucket_slots(owners):
    same = owners[..., :, None] == owners[..., None, :]
    count = owners.shape[-1]
    earlier = jnp.arange(count)[None, :] < jnp.arange(count)[:, None]
    ranks = lax.optimization_barrier(jnp.sum(jnp.logical_and(same, earlier).astype(jnp.int32), axis=-1)).astype(jnp.int32)
    return (owners * CAP + ranks).astype(jnp.int32)

def adam_update(first, second, grad_rows):
    new_first = 0.9 * first + 0.1 * grad_rows
    new_second = 0.999 * second + 0.001 * grad_rows * grad_rows
    scaled = 6.0 * (new_first / (1.0 - 0.9 ** 10)) / (jnp.sqrt(new_second / (1.0 - 0.999 ** 10)) + 1e-08)
    return (new_first, new_second, scaled.astype(jnp.bfloat16))

def reference(grads, raw_proj, bucket_owner, first_moment, second_moment):
    basis = cholesky_basis(raw_proj)
    blocks = D // BROWS // NB

    def accumulate(total, replica):
        return (total + replica.astype(jnp.float32), None)
    summed, _ = lax.scan(accumulate, jnp.zeros(grads.shape[1:], jnp.float32), grads)
    projected = jnp.einsum('mdk,mkr->mdr', summed, basis.astype(jnp.float32), precision=lax.Precision.HIGHEST)
    grad_rows = projected.reshape(MATS, blocks, NB, BROWS, R)
    slots = bucket_slots(bucket_owner.reshape(MATS, blocks, NB))
    mat_index = jnp.arange(MATS)[:, None, None]
    block_index = jnp.arange(blocks)[None, :, None]
    first = first_moment[mat_index, block_index, slots]
    second = second_moment[mat_index, block_index, slots]
    new_first, new_second, update = adam_update(first, second, grad_rows)
    delta = jnp.einsum('mcnbr,mkr->mcnbk', update.astype(jnp.float32), basis.astype(jnp.float32), precision=lax.Precision.HIGHEST)
    weight_delta = delta.astype(jnp.bfloat16).reshape(MATS, D, KV)
    first_out = first_moment.at[mat_index, block_index, slots].set(new_first)
    second_out = second_moment.at[mat_index, block_index, slots].set(new_second)
    return (weight_delta, first_out, second_out)
```

```python
import jax
import jax.numpy as jnp
from jax import lax
from jax.experimental import pallas as pl
from jax.experimental.pallas import tpu as pltpu
from jax.sharding import PartitionSpec as P

HI = lax.Precision.HIGHEST
F32 = jnp.float32
BF16 = jnp.bfloat16
BLK = 128
NZ, NY, CAP, ROWS = 8, 4, 4, 16


def mm(a, b, ca, cb, precision=HI):
    return lax.dot_general(
        a, b, (((ca,), (cb,)), ((), ())), precision=precision, preferred_element_type=F32
    )


def panel(S, g):
    rows = pl.ds(pl.multiple_of(8 * g, 8), 8)
    V, W = S[rows, 0:BLK], S[rows, BLK : 2 * BLK]
    turned = pltpu.roll(V, lax.rem(BLK - 8 * g, BLK), 1)
    C = [jnp.broadcast_to(turned[:, k : k + 1], (8, BLK)) for k in range(8)]
    sub = lax.broadcasted_iota(jnp.int32, (8, BLK), 0)
    lane = lax.broadcasted_iota(jnp.int32, (8, BLK), 1)
    pivot = jnp.ones((8, BLK), F32)
    for j in range(8):
        p = jnp.broadcast_to(C[j][j : j + 1, :], (8, BLK))
        pivot = jnp.where(sub == j, p, pivot)
        if j < 7:
            m = jnp.where(sub > j, C[j] * (1.0 / p), 0.0)
            for k in range(j + 1, 8):
                C[k] = C[k] - m * jnp.broadcast_to(C[k][j : j + 1, :], (8, BLK))
            V = V - m * jnp.broadcast_to(V[j : j + 1, :], (8, BLK))
            W = W - m * jnp.broadcast_to(W[j : j + 1, :], (8, BLK))
    s = lax.rsqrt(pivot)
    s = s * (1.5 - 0.5 * pivot * s * s)
    VW = jnp.concatenate([V * s, W * s], axis=1)
    S[rows, :] = VW
    later = jnp.where(lane >= 8 * g + 8, VW[:, 0:BLK], 0.0)
    S[...] = S[...] - mm(later, VW, 0, 0)


def factor(A, X, S, Q, hooks):
    eye = (
        lax.broadcasted_iota(jnp.int32, (BLK, BLK), 0)
        == lax.broadcasted_iota(jnp.int32, (BLK, BLK), 1)
    ).astype(F32)
    blocks = A.shape[0] // BLK
    for k in range(blocks):
        lo, hi = BLK * k, BLK * k + BLK
        S[:, 0:BLK] = A[lo:hi, lo:hi]
        S[:, BLK : 2 * BLK] = eye

        @pl.loop(0, BLK // 8)
        def _(g):
            panel(S, g)
            for at, hook in hooks.get(k, {}).items():
                pl.when(g == at)(hook)

        inverse = S[:, BLK : 2 * BLK]
        q = mm(X[:, lo:hi], inverse, 1, 1)
        Q[:, lo:hi] = q.astype(BF16)
        if k < blocks - 1:
            U = mm(inverse, A[lo:hi, hi:], 1, 0)
            A[hi:, hi:] = A[hi:, hi:] - mm(U, U, 0, 0)
            X[:, hi:] = X[:, hi:] - mm(q, U, 1, 0)


def scaled_update(first, second, g):
    new_first = 0.9 * first + 0.1 * g
    new_second = 0.999 * second + 0.001 * g * g
    scaled = 6.0 * (new_first / (1.0 - 0.9**10)) / (jnp.sqrt(new_second / (1.0 - 0.999**10)) + 1e-08)
    return scaled.astype(BF16)


def kernel(
    slots, bucket_of, grads, raw, first, second, basis_out, update_out, rows_out,
    X, A, S, Q, G, T, RA, RB, SA, SB, XS, XR, GS, MM, PR, U, GR, MT, GT,
    loc, ys, yr, tws, twr, mzs, mzr, mxs, mxr, rs, rr, xs, xr, gs, gr, es, er,
):
    dp, f = lax.axis_index("dp"), lax.axis_index("fsdp")
    z, xl, c = dp // 4, lax.rem(dp // 2, 2), lax.rem(dp, 2)
    xh, y = f // NY, lax.rem(f, NY)
    d = 1 - 2 * c

    def zat(k):
        return lax.rem(z + d * k + 2 * NZ, NZ)

    def at_z(k):
        return (zat(k) * 4 + xl * 2 + c, f)

    ahead, behind = at_z(1), at_z(-1)
    across = (z * 4 + (1 - xl) * 2 + c, f)
    twin = (z * 4 + xl * 2 + 1 - c, f)
    up, down = (dp, xh * NY + lax.rem(y + 1, NY)), (dp, xh * NY + lax.rem(y + NY - 1, NY))
    mirror = (z * 4 + (1 - xl) * 2 + c, (1 - xh) * NY + y)

    def remote(src, dst, send, recv, to):
        return pltpu.make_async_remote_copy(
            src_ref=src, dst_ref=dst, send_sem=send, recv_sem=recv,
            device_id=to, device_id_type=pl.DeviceIdType.MESH,
        )

    def fblock(h, yy, lo=0, n=128):
        return X.at[pl.ds(pl.multiple_of((h * NY + lax.rem(yy + 2 * NY, NY)) * 128 + lo, 64), n), :]

    def y_send(i):
        what = [
            (fblock(xh, y), up), (fblock(xh, y), down), (fblock(xh, y), mirror),
            (fblock(1 - xh, y), up), (fblock(1 - xh, y), down),
            (fblock(xh, y - 1, 0, 64), up), (fblock(xh, y + 1, 64, 64), down),
            (fblock(1 - xh, y - 1, 0, 64), up), (fblock(1 - xh, y + 1, 64, 64), down),
        ][i]
        return remote(what[0], what[0], ys.at[i], yr.at[i], what[1])

    def y_recv(i):
        what = [
            fblock(xh, y - 1), fblock(xh, y + 1), fblock(1 - xh, y),
            fblock(1 - xh, y - 1), fblock(1 - xh, y + 1),
            fblock(xh, y - 2, 0, 64), fblock(xh, y + 2, 64, 64),
            fblock(1 - xh, y - 2, 0, 64), fblock(1 - xh, y + 2, 64, 64),
        ][i]
        remote(what, what, ys.at[i], yr.at[i], up).wait_recv()

    def mblock(k, h):
        return MM.at[pl.ds(pl.multiple_of(zat(k) * 16 + h * 8, 8), 8)]

    def mz(s, way, k):
        i = s if way > 0 else 4 + s
        return remote(mblock(k, xl), mblock(k, xl), mzs.at[i], mzr.at[i], ahead if way > 0 else behind)

    def mx(i, k):
        return remote(mblock(k, xl), mblock(k, xl), mxs.at[i], mxr.at[i], across)

    def mx_recv(i, k):
        remote(mblock(k, 1 - xl), mblock(k, 1 - xl), mxs.at[i], mxr.at[i], across).wait_recv()

    def m_start():
        mz(0, 1, 0).start()
        mz(0, -1, 0).start()
        mx(0, 0).start()

    def m_step(s):
        mz(s - 1, 1, -s).wait_recv()
        if s < 4:
            mz(s, 1, -s).start()
        mx(s, -s).start()
        if s < 4:
            mz(s - 1, -1, s).wait_recv()
            if s < 3:
                mz(s, -1, s).start()
            mx(4 + s, s).start()

    def own(k):
        rows = pl.ds(pl.multiple_of(zat(k) * 128, 128), 128)
        return G[rows, :].astype(F32) + T[rows, :].astype(F32)

    def ra(s):
        return remote(SA if s == 0 else RA.at[s - 1], RA.at[s], rs.at[s], rr.at[s], ahead)

    def rb(s):
        return remote(SB if s == 0 else RB.at[s - 1], RB.at[s], rs.at[4 + s], rr.at[4 + s], behind)

    def r_start():
        SA[...] = own(4).astype(BF16)
        ra(0).start()
        SB[...] = own(-3).astype(BF16)
        rb(0).start()

    def r_step(s):
        ra(s - 1).wait_recv()
        RA[s - 1] = (RA[s - 1].astype(F32) + own(4 - s)).astype(BF16)
        ra(s).start()
        if s < 3:
            rb(s - 1).wait_recv()
            RB[s - 1] = (RB[s - 1].astype(F32) + own(s - 3)).astype(BF16)
            rb(s).start()

    x_sum = remote(XS, XR, xs, xr, across)

    def r_last():
        ra(3).wait_recv()
        rb(2).wait_recv()
        XS[...] = (own(0) + (RA[3].astype(F32) + RB[2].astype(F32))).astype(BF16)
        x_sum.start()

    def gblock(k):
        return GS.at[pl.ds(pl.multiple_of(zat(k) * 128, 128), 128), :]

    def gz(s, way, k):
        i = s if way > 0 else 4 + s
        return remote(gblock(k), gblock(k), gs.at[i], gr.at[i], ahead if way > 0 else behind)

    def g_start():
        x_sum.wait_recv()
        GS[pl.ds(pl.multiple_of(z * 128, 128), 128), :] = (
            XS[...].astype(F32) + XR[...].astype(F32)
        ).astype(BF16)
        gz(0, 1, 0).start()
        gz(0, -1, 0).start()

    def g_step(s):
        gz(s - 1, 1, -s).wait_recv()
        if s < 4:
            gz(s, 1, -s).start()
            gz(s - 1, -1, s).wait_recv()
            if s < 3:
                gz(s, -1, s).start()

    partners = (ahead, behind, across, twin, up, down, mirror)
    barrier = pltpu.get_barrier_semaphore()
    for to in partners:
        pl.semaphore_signal(barrier, inc=1, device_id=to, device_id_type=pl.DeviceIdType.MESH)
    own_raw = pltpu.make_async_copy(raw.at[c], fblock(xh, y), loc.at[0])
    own_grads = pltpu.make_async_copy(grads.at[0, c], G, loc.at[1])
    own_raw.start()
    own_grads.start()
    mine = pl.ds(pl.multiple_of(dp * CAP, CAP), CAP)
    MM[mine, 0] = first[c, 0].astype(BF16)
    MM[mine, 1] = second[c, 0].astype(BF16)
    MT[:, 0] = first[1 - c, 0].astype(BF16)
    MT[:, 1] = second[1 - c, 0].astype(BF16)
    own_raw.wait()
    pl.semaphore_wait(barrier, len(partners))

    for i in range(3):
        y_send(i).start()
    t_moments = remote(MT, MM.at[mine], tws.at[0], twr.at[0], twin)
    t_moments.start()
    t_grads = remote(grads.at[0, 1 - c], T, tws.at[1], twr.at[1], twin)
    t_grads.start()
    theirs = MM.at[pl.ds(pl.multiple_of((dp + 1 - 2 * c) * CAP, CAP), CAP)]
    own_grads.wait()
    t_grads.wait_recv()
    r_start()
    remote(MT, theirs, tws.at[0], twr.at[0], twin).wait_recv()
    m_start()

    y_recv(2)
    y_send(3).start()
    y_send(4).start()

    def gram(h, yy):
        part = fblock(h, yy)[...]
        return mm(part, part, 0, 0)

    A[...] = gram(xh, y) + gram(1 - xh, y)
    y_recv(0)
    y_send(5).start()
    y_recv(1)
    y_send(6).start()
    A[...] = A[...] + (gram(xh, y - 1) + gram(xh, y + 1))
    r_step(1)
    y_recv(3)
    y_send(7).start()
    y_recv(4)
    y_send(8).start()
    A[...] = A[...] + (gram(1 - xh, y - 1) + gram(1 - xh, y + 1))
    m_step(1)
    for i in range(5, 9):
        y_recv(i)
    A[...] = A[...] + (gram(xh, y + 2) + gram(1 - xh, y + 2))
    for i in range(9):
        y_send(i).wait_send()

    hooks = {
        0: {3: lambda: r_step(2), 8: lambda: m_step(2), 14: lambda: r_step(3)},
        1: {3: lambda: m_step(3), 8: r_last, 12: g_start, 15: lambda: m_step(4)},
        2: {6: lambda: g_step(1), 14: lambda: g_step(2)},
        3: {6: lambda: g_step(3)},
    }
    factor(A, X, S, Q, hooks)

    b_own = pltpu.make_async_copy(Q, basis_out.at[c], loc.at[2])
    b_twin = remote(Q, basis_out.at[c], es.at[0], er.at[0], twin)
    b_own.start()
    b_twin.start()
    g_step(4)
    for i in range(8):
        mx_recv(i, -i if i <= 4 else i - 4)

    pieces, height = 4, 256

    def u_own(i):
        part = pl.ds(i * height, height)
        return pltpu.make_async_copy(U.at[part, :], update_out.at[c, part, :], loc.at[3 + i])

    def u_twin(i):
        part = pl.ds(i * height, height)
        return remote(U.at[part, :], update_out.at[c, part, :], es.at[1 + i], er.at[1 + i], twin)

    for i in range(pieces):
        part, count = pl.ds(i * height, height), height // ROWS
        PR[i * count : (i + 1) * count] = mm(GS[part, :], Q[...], 1, 0, None).reshape(
            count, ROWS, PR.shape[2]
        )

        @pl.loop(i * count, (i + 1) * count)
        def _(b):
            rows = pl.ds(pl.multiple_of(b * ROWS, ROWS), ROWS)
            moments = MM[slots[c, b]]
            U[rows, :] = scaled_update(moments[0].astype(F32), moments[1].astype(F32), PR[b])

        u_own(i).start()
        u_twin(i).start()

    for i in range(CAP):
        GR[i] = PR[bucket_of[c, dp * CAP + i]]
        GT[i] = PR[bucket_of[c, (dp + 1 - 2 * c) * CAP + i]]
    r_own = pltpu.make_async_copy(GR, rows_out.at[c], loc.at[7])
    r_twin = remote(GT, rows_out.at[c], es.at[5], er.at[5], twin)
    r_own.start()
    r_twin.start()

    b_own.wait()
    r_own.wait()
    for i in range(pieces):
        u_own(i).wait()
        u_twin(i).wait_send()
    b_twin.wait_send()
    r_twin.wait_send()
    other = 1 - c
    remote(Q, basis_out.at[other], es.at[0], er.at[0], twin).wait_recv()
    remote(GT, rows_out.at[other], es.at[5], er.at[5], twin).wait_recv()
    for i in range(pieces):
        part = pl.ds(i * height, height)
        remote(U.at[part, :], update_out.at[other, part, :], es.at[1 + i], er.at[1 + i], twin).wait_recv()
    t_moments.wait_send()
    t_grads.wait_send()
    x_sum.wait_send()
    for s in range(4):
        ra(s).wait_send()
        mz(s, 1, -s).wait_send()
        gz(s, 1, -s).wait_send()
    for s in range(3):
        rb(s).wait_send()
        mz(s, -1, s).wait_send()
        gz(s, -1, s).wait_send()
    for i in range(8):
        mx(i, -i if i <= 4 else i - 4).wait_send()


def shards(grads, raw_proj, bucket_owner, first_moment, second_moment):
    matrices, local_rows, features = grads.shape[1:]
    rank = raw_proj.shape[2]
    buckets = bucket_owner.shape[1]
    capacity = first_moment.shape[2]
    slot_total = lax.axis_size("dp") * capacity
    same = bucket_owner[:, :, None] == bucket_owner[:, None, :]
    earlier = jnp.arange(buckets)[None, :] < jnp.arange(buckets)[:, None]
    ranks = jnp.sum(jnp.logical_and(same, earlier).astype(jnp.int32), axis=-1)
    slots = bucket_owner * capacity + ranks
    matches = slots[:, None, :] == jnp.arange(slot_total, dtype=jnp.int32)[None, :, None]
    occupied = jnp.any(matches, axis=2)
    bucket_of = jnp.sum(
        matches.astype(jnp.int32) * jnp.arange(buckets, dtype=jnp.int32)[None, None, :], axis=2
    )
    smem = pl.BlockSpec(memory_space=pltpu.SMEM)
    vmem = pl.BlockSpec(memory_space=pltpu.VMEM)
    anywhere = pl.BlockSpec(memory_space=pl.ANY)
    piece = (local_rows // NZ, features)
    dma = pltpu.SemaphoreType.DMA
    basis, update, grad_rows = pl.pallas_call(
        kernel,
        out_shape=(
            jax.ShapeDtypeStruct((matrices, features, rank), BF16),
            jax.ShapeDtypeStruct((matrices, local_rows, rank), BF16),
            jax.ShapeDtypeStruct((matrices, capacity, ROWS, rank), F32),
        ),
        in_specs=[smem, smem, anywhere, anywhere, vmem, vmem],
        out_specs=(anywhere, anywhere, anywhere),
        scratch_shapes=[
            pltpu.VMEM((features, rank), F32),
            pltpu.VMEM((rank, rank), F32),
            pltpu.VMEM((BLK, 2 * BLK), F32),
            pltpu.VMEM((features, rank), BF16),
            pltpu.VMEM((local_rows, features), BF16),
            pltpu.VMEM((local_rows, features), BF16),
            pltpu.VMEM((4, *piece), BF16),
            pltpu.VMEM((3, *piece), BF16),
            pltpu.VMEM(piece, BF16),
            pltpu.VMEM(piece, BF16),
            pltpu.VMEM(piece, BF16),
            pltpu.VMEM(piece, BF16),
            pltpu.VMEM((local_rows, features), BF16),
            pltpu.VMEM((slot_total, 2, ROWS, rank), BF16),
            pltpu.VMEM((buckets, ROWS, rank), F32),
            pltpu.VMEM((local_rows, rank), BF16),
            pltpu.VMEM((capacity, ROWS, rank), F32),
            pltpu.VMEM((capacity, 2, ROWS, rank), BF16),
            pltpu.VMEM((capacity, ROWS, rank), F32),
            dma((8,)), dma((9,)), dma((9,)), dma((2,)), dma((2,)),
            dma((7,)), dma((7,)), dma((8,)), dma((8,)), dma((7,)), dma((7,)),
            dma, dma, dma((7,)), dma((7,)), dma((6,)), dma((6,)),
        ],
        compiler_params=pltpu.CompilerParams(
            collective_id=0, has_side_effects=True, vmem_limit_bytes=52 << 20
        ),
        cost_estimate=pl.CostEstimate(
            flops=10_000_000_000, bytes_accessed=16_000_000, transcendentals=1_000_000
        ),
    )(slots, bucket_of, grads, raw_proj, first_moment, second_moment)
    start = lax.axis_index("dp") * capacity
    keep = lax.dynamic_slice_in_dim(occupied, start, capacity, 1)[:, :, None, None]
    first, second = first_moment[:, 0], second_moment[:, 0]
    first_out = jnp.where(keep, 0.9 * first + 0.1 * grad_rows, first)[:, None]
    second_out = jnp.where(keep, 0.999 * second + 0.001 * grad_rows * grad_rows, second)[:, None]
    weight_delta = jnp.einsum(
        "mdr,mkr->mdk", update, basis, preferred_element_type=F32
    ).astype(BF16)
    return (weight_delta, first_out, second_out)


def solution(mesh):
    return jax.shard_map(
        shards,
        mesh=mesh,
        in_specs=(
            P("dp", None, "fsdp", None),
            P(None, "fsdp", None),
            P(None, "fsdp"),
            P(None, "fsdp", "dp", None, None),
            P(None, "fsdp", "dp", None, None),
        ),
        out_specs=(
            P(None, "fsdp", None),
            P(None, "fsdp", "dp", None, None),
            P(None, "fsdp", "dp", None, None),
        ),
        check_vma=False,
    )
```

```python
import jax
import jax.numpy as jnp
from jax import lax
from jax.experimental import pallas as pl
from jax.experimental.pallas import tpu as pltpu
from jax.sharding import PartitionSpec as P

HI = lax.Precision.HIGHEST
F32 = jnp.float32
BF16 = jnp.bfloat16
BLK = 128
PAN = 16
NZ, NY, CAP, ROWS = 8, 4, 4, 16


def mm(a, b, ca, cb, precision=HI):
    return lax.dot_general(
        a, b, (((ca,), (cb,)), ((), ())), precision=precision, preferred_element_type=F32
    )


def split(x):
    high = x.astype(BF16).astype(F32)
    middle = (x - high).astype(BF16).astype(F32)
    return high, middle, (x - high) - middle


def mm3(a, b, ca, cb):
    ah, bh = a.astype(BF16), b.astype(BF16)
    al, bl = (a - ah.astype(F32)).astype(BF16), (b - bh.astype(F32)).astype(BF16)
    return mm(ah, bh, ca, cb, None) + (mm(ah, bl, ca, cb, None) + mm(al, bh, ca, cb, None))


def panel(S, g):
    rows = pl.ds(pl.multiple_of(PAN * g, PAN), PAN)
    V, W = S[rows, 0:BLK], S[rows, BLK : 2 * BLK]
    turned = pltpu.roll(V, lax.rem(BLK - PAN * g, BLK), 1)
    C = [jnp.broadcast_to(turned[:, k : k + 1], (PAN, BLK)) for k in range(PAN)]
    sub = lax.broadcasted_iota(jnp.int32, (PAN, BLK), 0)
    lane = lax.broadcasted_iota(jnp.int32, (PAN, BLK), 1)
    pivot = jnp.ones((PAN, BLK), F32)
    for j in range(PAN):
        p = C[j][j : j + 1, :]
        pivot = jnp.where(sub == j, jnp.broadcast_to(p, (PAN, BLK)), pivot)
        if j < PAN - 1:
            m = jnp.where(sub > j, C[j] * jnp.broadcast_to(1.0 / p, (PAN, BLK)), 0.0)
            for k in range(j + 1, PAN):
                C[k] = C[k] - m * jnp.broadcast_to(C[k][j : j + 1, :], (PAN, BLK))
            V = V - m * jnp.broadcast_to(V[j : j + 1, :], (PAN, BLK))
            W = W - m * jnp.broadcast_to(W[j : j + 1, :], (PAN, BLK))
    s = lax.rsqrt(pivot)
    s = s * (1.5 - 0.5 * pivot * s * s)
    VW = jnp.concatenate([V * s, W * s], axis=1)
    S[rows, :] = VW
    high, middle, low = split(VW)
    h, m, l = (jnp.where(lane >= PAN * (g + 1), x[:, 0:BLK], 0.0) for x in (high, middle, low))
    left = jnp.concatenate([h, h, m, h, l, m], axis=0).astype(BF16)
    right = jnp.concatenate([high, middle, high, low, high, middle], axis=0).astype(BF16)
    S[...] = S[...] - mm(left, right, 0, 0, None)


def factor(A, X, S, Q, hooks):
    eye = (
        lax.broadcasted_iota(jnp.int32, (BLK, BLK), 0)
        == lax.broadcasted_iota(jnp.int32, (BLK, BLK), 1)
    ).astype(F32)
    blocks = A.shape[0] // BLK
    for k in range(blocks):
        lo, hi = BLK * k, BLK * k + BLK
        S[:, 0:BLK] = A[lo:hi, lo:hi]
        S[:, BLK : 2 * BLK] = eye

        @pl.loop(0, BLK // PAN)
        def _(g):
            panel(S, g)
            for at, hook in hooks.get(k, {}).items():
                pl.when(g == at)(hook)

        inverse = S[:, BLK : 2 * BLK]
        q = mm3(X[:, lo:hi], inverse, 1, 1)
        Q[:, lo:hi] = q.astype(BF16)
        if k < blocks - 1:
            U = mm(inverse, A[lo:hi, hi:], 1, 0)
            A[hi:, hi:] = A[hi:, hi:] - mm(U, U, 0, 0)
            X[:, hi:] = X[:, hi:] - mm3(q, U, 1, 0)


def scaled_update(first, second, g):
    new_first = 0.9 * first + 0.1 * g
    new_second = 0.999 * second + 0.001 * g * g
    scaled = 6.0 * (new_first / (1.0 - 0.9**10)) / (jnp.sqrt(new_second / (1.0 - 0.999**10)) + 1e-08)
    return scaled.astype(BF16)


def kernel(
    slots, bucket_of, grads, raw, first, second, basis_out, update_out, rows_out,
    X, A, S, Q, G, T, RA, RB, SA, SB, XS, XR, MM, MO, PB, U, GR, MT, GT,
    loc, uo, us, ur, ys, yr, tws, twr, mzs, mzr, mxs, mxr, rs, rr, xs, xr, gs, gr, es, er,
):
    dp, f = lax.axis_index("dp"), lax.axis_index("fsdp")
    z, xl, c = dp // 4, lax.rem(dp // 2, 2), lax.rem(dp, 2)
    xh, y = f // NY, lax.rem(f, NY)
    d = 1 - 2 * c

    def zat(k):
        return lax.rem(z + d * k + 2 * NZ, NZ)

    def at_z(k):
        return (zat(k) * 4 + xl * 2 + c, f)

    ahead, behind = at_z(1), at_z(-1)
    across = (z * 4 + (1 - xl) * 2 + c, f)
    twin = (z * 4 + xl * 2 + 1 - c, f)
    up, down = (dp, xh * NY + lax.rem(y + 1, NY)), (dp, xh * NY + lax.rem(y + NY - 1, NY))
    mirror = (z * 4 + (1 - xl) * 2 + c, (1 - xh) * NY + y)

    def remote(src, dst, send, recv, to):
        return pltpu.make_async_remote_copy(
            src_ref=src, dst_ref=dst, send_sem=send, recv_sem=recv,
            device_id=to, device_id_type=pl.DeviceIdType.MESH,
        )

    def fblock(h, yy, lo=0, n=128):
        return X.at[pl.ds(pl.multiple_of((h * NY + lax.rem(yy + 2 * NY, NY)) * 128 + lo, 64), n), :]

    def y_send(i):
        what = [
            (fblock(xh, y), up), (fblock(xh, y), down), (fblock(xh, y), mirror),
            (fblock(1 - xh, y), up), (fblock(1 - xh, y), down),
            (fblock(xh, y - 1, 0, 64), up), (fblock(xh, y + 1, 64, 64), down),
            (fblock(1 - xh, y - 1, 0, 64), up), (fblock(1 - xh, y + 1, 64, 64), down),
        ][i]
        return remote(what[0], what[0], ys.at[i], yr.at[i], what[1])

    def y_recv(i):
        what = [
            fblock(xh, y - 1), fblock(xh, y + 1), fblock(1 - xh, y),
            fblock(1 - xh, y - 1), fblock(1 - xh, y + 1),
            fblock(xh, y - 2, 0, 64), fblock(xh, y + 2, 64, 64),
            fblock(1 - xh, y - 2, 0, 64), fblock(1 - xh, y + 2, 64, 64),
        ][i]
        remote(what, what, ys.at[i], yr.at[i], up).wait_recv()

    def mblock(k, h):
        return MM.at[pl.ds(pl.multiple_of(zat(k) * 16 + h * 8, 8), 8)]

    def mz(s, way, k):
        i = s if way > 0 else 4 + s
        return remote(mblock(k, xl), mblock(k, xl), mzs.at[i], mzr.at[i], ahead if way > 0 else behind)

    def mx(i, k):
        return remote(mblock(k, xl), mblock(k, xl), mxs.at[i], mxr.at[i], across)

    def mx_recv(i, k):
        remote(mblock(k, 1 - xl), mblock(k, 1 - xl), mxs.at[i], mxr.at[i], across).wait_recv()

    def m_start():
        mz(0, 1, 0).start()
        mz(0, -1, 0).start()
        mx(0, 0).start()

    def m_step(s):
        mz(s - 1, 1, -s).wait_recv()
        if s < 4:
            mz(s, 1, -s).start()
        mx(s, -s).start()
        if s < 4:
            mz(s - 1, -1, s).wait_recv()
            if s < 3:
                mz(s, -1, s).start()
            mx(4 + s, s).start()

    def own(k):
        rows = pl.ds(pl.multiple_of(zat(k) * 128, 128), 128)
        return G[rows, :].astype(F32) + T[rows, :].astype(F32)

    def ra(s):
        return remote(SA if s == 0 else RA.at[s - 1], RA.at[s], rs.at[s], rr.at[s], ahead)

    def rb(s):
        return remote(SB if s == 0 else RB.at[s - 1], RB.at[s], rs.at[4 + s], rr.at[4 + s], behind)

    def r_start():
        SA[...] = own(4).astype(BF16)
        ra(0).start()
        SB[...] = own(-3).astype(BF16)
        rb(0).start()

    def r_step(s):
        ra(s - 1).wait_recv()
        RA[s - 1] = (RA[s - 1].astype(F32) + own(4 - s)).astype(BF16)
        ra(s).start()
        if s < 3:
            rb(s - 1).wait_recv()
            RB[s - 1] = (RB[s - 1].astype(F32) + own(s - 3)).astype(BF16)
            rb(s).start()

    x_sum = remote(XS, XR, xs, xr, across)

    def r_sum():
        x_sum.wait_recv()
        x_sum.wait_send()
        XS[...] = (XS[...].astype(F32) + XR[...].astype(F32)).astype(BF16)

    def r_last():
        ra(3).wait_recv()
        rb(2).wait_recv()
        XS[...] = (own(0) + (RA[3].astype(F32) + RB[2].astype(F32))).astype(BF16)
        x_sum.start()

    def pblock(k):
        return PB.at[pl.ds(pl.multiple_of(zat(k) * 8, 8), 8)]

    def gz(s, way, k):
        i = s if way > 0 else 4 + s
        return remote(pblock(k), pblock(k), gs.at[i], gr.at[i], ahead if way > 0 else behind)

    def g_start():
        part = mm(XS[...], Q[...], 1, 0, None)
        pblock(0)[...] = part.reshape(8, ROWS, part.shape[1]).astype(BF16)
        gz(0, 1, 0).start()
        gz(0, -1, 0).start()

    def g_step(s):
        gz(s - 1, 1, -s).wait_recv()
        if s < 4:
            gz(s, 1, -s).start()
            gz(s - 1, -1, s).wait_recv()
            if s < 3:
                gz(s, -1, s).start()

    partners = (ahead, behind, across, twin, up, down, mirror)
    barrier = pltpu.get_barrier_semaphore()
    for to in partners:
        pl.semaphore_signal(barrier, inc=1, device_id=to, device_id_type=pl.DeviceIdType.MESH)
    own_raw = pltpu.make_async_copy(raw.at[c], fblock(xh, y), loc.at[0])
    own_grads = pltpu.make_async_copy(grads.at[0, c], G, loc.at[1])
    own_raw.start()
    own_grads.start()
    own_moments = [
        pltpu.make_async_copy(ref, MO.at[i], loc.at[2 + i]) for i, ref in enumerate((first, second))
    ]
    for copy in own_moments:
        copy.start()
    mine = pl.ds(pl.multiple_of(dp * CAP, CAP), CAP)
    for i, copy in enumerate(own_moments):
        copy.wait()
        MM[mine, i] = MO[i, c, 0].astype(BF16)
        MT[:, i] = MO[i, 1 - c, 0].astype(BF16)
    own_raw.wait()
    pl.semaphore_wait(barrier, len(partners))

    for i in range(3):
        y_send(i).start()
    t_moments = remote(MT, MM.at[mine], tws.at[0], twr.at[0], twin)
    t_moments.start()
    t_grads = remote(grads.at[0, 1 - c], T, tws.at[1], twr.at[1], twin)
    t_grads.start()
    theirs = MM.at[pl.ds(pl.multiple_of((dp + 1 - 2 * c) * CAP, CAP), CAP)]
    own_grads.wait()
    t_grads.wait_recv()
    r_start()
    remote(MT, theirs, tws.at[0], twr.at[0], twin).wait_recv()
    m_start()

    y_recv(2)
    y_send(3).start()
    y_send(4).start()

    def gram(h, yy):
        part = fblock(h, yy)[...]
        return mm(part, part, 0, 0)

    A[...] = gram(xh, y) + gram(1 - xh, y)
    y_recv(0)
    y_send(5).start()
    y_recv(1)
    y_send(6).start()
    A[...] = A[...] + (gram(xh, y - 1) + gram(xh, y + 1))
    r_step(1)
    y_recv(3)
    y_send(7).start()
    y_recv(4)
    y_send(8).start()
    A[...] = A[...] + (gram(1 - xh, y - 1) + gram(1 - xh, y + 1))
    m_step(1)
    for i in range(5, 9):
        y_recv(i)
    A[...] = A[...] + (gram(xh, y + 2) + gram(1 - xh, y + 2))
    for i in range(9):
        y_send(i).wait_send()

    hooks = {
        0: {2: lambda: r_step(2), 6: lambda: m_step(2)},
        1: {2: lambda: r_step(3), 6: lambda: m_step(3)},
        2: {5: r_last},
        3: {2: lambda: m_step(4), 6: r_sum},
    }
    factor(A, X, S, Q, hooks)
    g_start()

    b_own = pltpu.make_async_copy(Q, basis_out.at[c], loc.at[4])
    b_twin = remote(Q, basis_out.at[c], es.at[0], er.at[0], twin)
    b_own.start()
    b_twin.start()
    for i in range(8):
        mx_recv(i, -i if i <= 4 else i - 4)

    def urows(k):
        return pl.ds(pl.multiple_of(zat(k) * 128, 128), 128)

    def u_own(i, k):
        return pltpu.make_async_copy(U.at[urows(k), :], update_out.at[c, urows(k), :], uo.at[i])

    def u_twin(i, k, at):
        return remote(U.at[urows(k), :], update_out.at[at, urows(k), :], us.at[i], ur.at[i], twin)

    def update(i, k):
        @pl.loop(0, 8)
        def _(j):
            b = zat(k) * 8 + j
            moments = MM[slots[c, b]]
            U[pl.ds(pl.multiple_of(b * ROWS, ROWS), ROWS), :] = scaled_update(
                moments[0].astype(F32), moments[1].astype(F32), PB[b].astype(F32)
            )

        u_own(i, k).start()
        u_twin(i, k, c).start()

    order = (0, -1, 1, -2, 2, -3, 3, 4)
    update(0, 0)
    for s in range(1, 4):
        g_step(s)
        update(2 * s - 1, -s)
        update(2 * s, s)
    g_step(4)
    update(7, 4)

    for i in range(CAP):
        GR[i] = PB[bucket_of[c, dp * CAP + i]].astype(F32)
        GT[i] = PB[bucket_of[c, (dp + 1 - 2 * c) * CAP + i]].astype(F32)
    r_own = pltpu.make_async_copy(GR, rows_out.at[c], loc.at[5])
    r_twin = remote(GT, rows_out.at[c], es.at[1], er.at[1], twin)
    r_own.start()
    r_twin.start()

    other = 1 - c
    for i, k in enumerate(order):
        u_own(i, k).wait()
        u_twin(i, k, c).wait_send()
    for i, k in enumerate(order):
        u_twin(i, -k, other).wait_recv()
    b_own.wait()
    r_own.wait()
    b_twin.wait_send()
    r_twin.wait_send()
    remote(Q, basis_out.at[other], es.at[0], er.at[0], twin).wait_recv()
    remote(GT, rows_out.at[other], es.at[1], er.at[1], twin).wait_recv()
    t_moments.wait_send()
    t_grads.wait_send()
    for s in range(4):
        ra(s).wait_send()
        mz(s, 1, -s).wait_send()
        gz(s, 1, -s).wait_send()
    for s in range(3):
        rb(s).wait_send()
        mz(s, -1, s).wait_send()
        gz(s, -1, s).wait_send()
    for i in range(8):
        mx(i, -i if i <= 4 else i - 4).wait_send()


def delta_kernel(update, basis, out):
    out[0] = mm(update[0], basis[0], 1, 1, None).astype(BF16)


def shards(grads, raw_proj, bucket_owner, first_moment, second_moment):
    matrices, local_rows, features = grads.shape[1:]
    rank = raw_proj.shape[2]
    buckets = bucket_owner.shape[1]
    capacity = first_moment.shape[2]
    slot_total = lax.axis_size("dp") * capacity
    same = bucket_owner[:, :, None] == bucket_owner[:, None, :]
    earlier = jnp.arange(buckets)[None, :] < jnp.arange(buckets)[:, None]
    ranks = jnp.sum(jnp.logical_and(same, earlier).astype(jnp.int32), axis=-1)
    slots = bucket_owner * capacity + ranks
    matches = slots[:, None, :] == jnp.arange(slot_total, dtype=jnp.int32)[None, :, None]
    occupied = jnp.any(matches, axis=2)
    bucket_of = jnp.sum(
        matches.astype(jnp.int32) * jnp.arange(buckets, dtype=jnp.int32)[None, None, :], axis=2
    )
    smem = pl.BlockSpec(memory_space=pltpu.SMEM)
    anywhere = pl.BlockSpec(memory_space=pl.ANY)
    piece = (local_rows // NZ, features)
    dma = pltpu.SemaphoreType.DMA
    basis, update, grad_rows = pl.pallas_call(
        kernel,
        out_shape=(
            jax.ShapeDtypeStruct((matrices, features, rank), BF16),
            jax.ShapeDtypeStruct((matrices, local_rows, rank), BF16),
            jax.ShapeDtypeStruct((matrices, capacity, ROWS, rank), F32),
        ),
        in_specs=[smem, smem] + [anywhere] * 4,
        out_specs=(anywhere, anywhere, anywhere),
        scratch_shapes=[
            pltpu.VMEM((features, rank), F32),
            pltpu.VMEM((rank, rank), F32),
            pltpu.VMEM((BLK, 2 * BLK), F32),
            pltpu.VMEM((features, rank), BF16),
            pltpu.VMEM((local_rows, features), BF16),
            pltpu.VMEM((local_rows, features), BF16),
            pltpu.VMEM((4, *piece), BF16),
            pltpu.VMEM((3, *piece), BF16),
            pltpu.VMEM(piece, BF16),
            pltpu.VMEM(piece, BF16),
            pltpu.VMEM(piece, BF16),
            pltpu.VMEM(piece, BF16),
            pltpu.VMEM((slot_total, 2, ROWS, rank), BF16),
            pltpu.VMEM((2, *first_moment.shape), F32),
            pltpu.VMEM((buckets, ROWS, rank), BF16),
            pltpu.VMEM((local_rows, rank), BF16),
            pltpu.VMEM((capacity, ROWS, rank), F32),
            pltpu.VMEM((capacity, 2, ROWS, rank), BF16),
            pltpu.VMEM((capacity, ROWS, rank), F32),
            dma((6,)), dma((8,)), dma((8,)), dma((8,)), dma((9,)), dma((9,)), dma((2,)), dma((2,)),
            dma((7,)), dma((7,)), dma((8,)), dma((8,)), dma((7,)), dma((7,)),
            dma, dma, dma((7,)), dma((7,)), dma((2,)), dma((2,)),
        ],
        compiler_params=pltpu.CompilerParams(
            collective_id=0, has_side_effects=True, vmem_limit_bytes=56 << 20
        ),
        cost_estimate=pl.CostEstimate(
            flops=10_000_000_000, bytes_accessed=16_000_000, transcendentals=1_000_000
        ),
    )(slots, bucket_of, grads, raw_proj, first_moment, second_moment)
    start = lax.axis_index("dp") * capacity
    keep = lax.dynamic_slice_in_dim(occupied, start, capacity, 1)[:, :, None, None]
    first, second = first_moment[:, 0], second_moment[:, 0]
    first_out = jnp.where(keep, 0.9 * first + 0.1 * grad_rows, first)[:, None]
    second_out = jnp.where(keep, 0.999 * second + 0.001 * grad_rows * grad_rows, second)[:, None]
    height = 256
    weight_delta = pl.pallas_call(
        delta_kernel,
        out_shape=jax.ShapeDtypeStruct((matrices, local_rows, features), BF16),
        grid=(matrices, local_rows // height),
        in_specs=[
            pl.BlockSpec((1, height, rank), lambda m, i: (m, i, 0)),
            pl.BlockSpec((1, features, rank), lambda m, i: (m, 0, 0)),
        ],
        out_specs=pl.BlockSpec((1, height, features), lambda m, i: (m, i, 0)),
    )(update, basis)
    return (weight_delta, first_out, second_out)


def solution(mesh):
    return jax.shard_map(
        shards,
        mesh=mesh,
        in_specs=(
            P("dp", None, "fsdp", None),
            P(None, "fsdp", None),
            P(None, "fsdp"),
            P(None, "fsdp", "dp", None, None),
            P(None, "fsdp", "dp", None, None),
        ),
        out_specs=(
            P(None, "fsdp", None),
            P(None, "fsdp", "dp", None, None),
            P(None, "fsdp", "dp", None, None),
        ),
        check_vma=False,
    )
```

```python
import jax
import jax.numpy as jnp
from jax import lax
from jax.experimental import pallas as pl
from jax.experimental.pallas import tpu as pltpu
from jax.sharding import PartitionSpec as P

HI = lax.Precision.HIGHEST
F32 = jnp.float32
BF16 = jnp.bfloat16
BLK = 128
PAN = 16
NZ, NY, CAP, ROWS = 8, 4, 4, 16


def mm(a, b, ca, cb, precision=HI):
    return lax.dot_general(
        a, b, (((ca,), (cb,)), ((), ())), precision=precision, preferred_element_type=F32
    )


def split(x):
    high = x.astype(BF16).astype(F32)
    middle = (x - high).astype(BF16).astype(F32)
    return high, middle, (x - high) - middle


def mm3(a, b, ca, cb):
    ah, bh = a.astype(BF16), b.astype(BF16)
    al, bl = (a - ah.astype(F32)).astype(BF16), (b - bh.astype(F32)).astype(BF16)
    return mm(ah, bh, ca, cb, None) + (mm(ah, bl, ca, cb, None) + mm(al, bh, ca, cb, None))


def panel(S, g):
    rows = pl.ds(pl.multiple_of(PAN * g, PAN), PAN)
    V, W = S[rows, 0:BLK], S[rows, BLK : 2 * BLK]
    turned = pltpu.roll(V, lax.rem(BLK - PAN * g, BLK), 1)
    C = [jnp.broadcast_to(turned[:, k : k + 1], (PAN, BLK)) for k in range(PAN)]
    sub = lax.broadcasted_iota(jnp.int32, (PAN, BLK), 0)
    lane = lax.broadcasted_iota(jnp.int32, (PAN, BLK), 1)
    pivot = jnp.ones((PAN, BLK), F32)
    for j in range(PAN):
        p = C[j][j : j + 1, :]
        pivot = jnp.where(sub == j, jnp.broadcast_to(p, (PAN, BLK)), pivot)
        if j < PAN - 1:
            m = jnp.where(sub > j, C[j] * jnp.broadcast_to(1.0 / p, (PAN, BLK)), 0.0)
            for k in range(j + 1, PAN):
                C[k] = C[k] - m * jnp.broadcast_to(C[k][j : j + 1, :], (PAN, BLK))
            V = V - m * jnp.broadcast_to(V[j : j + 1, :], (PAN, BLK))
            W = W - m * jnp.broadcast_to(W[j : j + 1, :], (PAN, BLK))
    s = lax.rsqrt(pivot)
    s = s * (1.5 - 0.5 * pivot * s * s)
    VW = jnp.concatenate([V * s, W * s], axis=1)
    S[rows, :] = VW
    high, middle, low = split(VW)
    h, m, l = (jnp.where(lane >= PAN * (g + 1), x[:, 0:BLK], 0.0) for x in (high, middle, low))
    left = jnp.concatenate([h, h, m, h, l, m], axis=0).astype(BF16)
    right = jnp.concatenate([high, middle, high, low, high, middle], axis=0).astype(BF16)
    S[...] = S[...] - mm(left, right, 0, 0, None)


def factor(A, X, S, Q, hooks):
    eye = (
        lax.broadcasted_iota(jnp.int32, (BLK, BLK), 0)
        == lax.broadcasted_iota(jnp.int32, (BLK, BLK), 1)
    ).astype(F32)
    blocks = A.shape[0] // BLK
    for k in range(blocks):
        lo, hi = BLK * k, BLK * k + BLK
        S[:, 0:BLK] = A[lo:hi, lo:hi]
        S[:, BLK : 2 * BLK] = eye

        @pl.loop(0, BLK // PAN)
        def _(g):
            panel(S, g)
            for at, hook in hooks.get(k, {}).items():
                pl.when(g == at)(hook)

        inverse = S[:, BLK : 2 * BLK]
        q = mm3(X[:, lo:hi], inverse, 1, 1)
        Q[:, lo:hi] = q.astype(BF16)
        if k < blocks - 1:
            U = mm(inverse, A[lo:hi, hi:], 1, 0)
            A[hi:, hi:] = A[hi:, hi:] - mm(U, U, 0, 0)
            X[:, hi:] = X[:, hi:] - mm3(q, U, 1, 0)


def scaled_update(first, second, g):
    new_first = 0.9 * first + 0.1 * g
    new_second = 0.999 * second + 0.001 * g * g
    scaled = 6.0 * (new_first / (1.0 - 0.9**10)) / (jnp.sqrt(new_second / (1.0 - 0.999**10)) + 1e-08)
    return scaled.astype(BF16)


def kernel(
    slots, bucket_of, grads, raw, first, second, delta_out, rows_out,
    X, A, S, Q, QT, G, T, RA, RB, SA, SB, XS, XR, MM, MO, PB, U, D, GT, MT,
    loc, do, ds, dr, us, ur, ys, yr, tws, twr, mzs, mzr, rs, rr, xs, xr, gs, gr, es, er,
):
    dp, f = lax.axis_index("dp"), lax.axis_index("fsdp")
    z, xl, c = dp // 4, lax.rem(dp // 2, 2), lax.rem(dp, 2)
    xh, y = f // NY, lax.rem(f, NY)
    d = 1 - 2 * c

    def zat(k):
        return lax.rem(z + d * k + 2 * NZ, NZ)

    def at_z(k):
        return (zat(k) * 4 + xl * 2 + c, f)

    ahead, behind = at_z(1), at_z(-1)
    across = (z * 4 + (1 - xl) * 2 + c, f)
    twin = (z * 4 + xl * 2 + 1 - c, f)
    diagonal = (z * 4 + (1 - xl) * 2 + 1 - c, f)
    half = Q.shape[1] // 2
    columns = pl.ds(pl.multiple_of(xl * half, half), half)
    others = pl.ds(pl.multiple_of((1 - xl) * half, half), half)
    up, down = (dp, xh * NY + lax.rem(y + 1, NY)), (dp, xh * NY + lax.rem(y + NY - 1, NY))
    mirror = (z * 4 + (1 - xl) * 2 + c, (1 - xh) * NY + y)

    def remote(src, dst, send, recv, to):
        return pltpu.make_async_remote_copy(
            src_ref=src, dst_ref=dst, send_sem=send, recv_sem=recv,
            device_id=to, device_id_type=pl.DeviceIdType.MESH,
        )

    def fblock(h, yy, lo=0, n=128):
        return X.at[pl.ds(pl.multiple_of((h * NY + lax.rem(yy + 2 * NY, NY)) * 128 + lo, 64), n), :]

    def y_send(i):
        what = [
            (fblock(xh, y), up), (fblock(xh, y), down), (fblock(xh, y), mirror),
            (fblock(1 - xh, y), up), (fblock(1 - xh, y), down),
            (fblock(xh, y - 1, 0, 64), up), (fblock(xh, y + 1, 64, 64), down),
            (fblock(1 - xh, y - 1, 0, 64), up), (fblock(1 - xh, y + 1, 64, 64), down),
        ][i]
        return remote(what[0], what[0], ys.at[i], yr.at[i], what[1])

    def y_recv(i):
        what = [
            fblock(xh, y - 1), fblock(xh, y + 1), fblock(1 - xh, y),
            fblock(1 - xh, y - 1), fblock(1 - xh, y + 1),
            fblock(xh, y - 2, 0, 64), fblock(xh, y + 2, 64, 64),
            fblock(1 - xh, y - 2, 0, 64), fblock(1 - xh, y + 2, 64, 64),
        ][i]
        remote(what, what, ys.at[i], yr.at[i], up).wait_recv()

    def mblock(k):
        return MM.at[pl.ds(pl.multiple_of(zat(k) * 16, 16), 16)]

    def mz(s, way, k):
        i = s if way > 0 else 4 + s
        return remote(mblock(k), mblock(k), mzs.at[i], mzr.at[i], ahead if way > 0 else behind)

    def m_start():
        mz(0, 1, 0).start()
        mz(0, -1, 0).start()

    def m_step(s):
        mz(s - 1, 1, -s).wait_recv()
        if s < 4:
            mz(s, 1, -s).start()
            mz(s - 1, -1, s).wait_recv()
            if s < 3:
                mz(s, -1, s).start()

    def own(k):
        rows = pl.ds(pl.multiple_of(zat(k) * 128, 128), 128)
        return G[rows, :].astype(F32) + T[rows, :].astype(F32)

    def ra(s):
        return remote(SA if s == 0 else RA.at[s - 1], RA.at[s], rs.at[s], rr.at[s], ahead)

    def rb(s):
        return remote(SB if s == 0 else RB.at[s - 1], RB.at[s], rs.at[4 + s], rr.at[4 + s], behind)

    def r_start():
        SA[...] = own(4).astype(BF16)
        ra(0).start()
        SB[...] = own(-3).astype(BF16)
        rb(0).start()

    def r_step(s):
        ra(s - 1).wait_recv()
        RA[s - 1] = (RA[s - 1].astype(F32) + own(4 - s)).astype(BF16)
        ra(s).start()
        if s < 3:
            rb(s - 1).wait_recv()
            RB[s - 1] = (RB[s - 1].astype(F32) + own(s - 3)).astype(BF16)
            rb(s).start()

    x_sum = remote(XS, XR, xs, xr, across)

    def r_sum():
        x_sum.wait_recv()
        x_sum.wait_send()
        XS[...] = (XS[...].astype(F32) + XR[...].astype(F32)).astype(BF16)

    def r_last():
        ra(3).wait_recv()
        rb(2).wait_recv()
        XS[...] = (own(0) + (RA[3].astype(F32) + RB[2].astype(F32))).astype(BF16)
        x_sum.start()

    def pblock(k):
        return PB.at[pl.ds(pl.multiple_of(zat(k) * 8, 8), 8)]

    def gz(s, way, k):
        i = s if way > 0 else 4 + s
        return remote(pblock(k), pblock(k), gs.at[i], gr.at[i], ahead if way > 0 else behind)

    def g_start():
        part = mm(XS[...], Q[:, columns], 1, 0, None)
        pblock(0)[...] = part.reshape(8, ROWS, part.shape[1]).astype(BF16)
        gz(0, 1, 0).start()
        gz(0, -1, 0).start()

    def g_step(s):
        gz(s - 1, 1, -s).wait_recv()
        if s < 4:
            gz(s, 1, -s).start()
            gz(s - 1, -1, s).wait_recv()
            if s < 3:
                gz(s, -1, s).start()

    partners = (ahead, behind, across, twin, diagonal, up, down, mirror)
    barrier = pltpu.get_barrier_semaphore()
    for to in partners:
        pl.semaphore_signal(barrier, inc=1, device_id=to, device_id_type=pl.DeviceIdType.MESH)
    own_raw = pltpu.make_async_copy(raw.at[c], fblock(xh, y), loc.at[0])
    own_grads = pltpu.make_async_copy(grads.at[0, c], G, loc.at[1])
    own_raw.start()
    own_grads.start()
    own_moments = [
        pltpu.make_async_copy(ref, MO.at[i], loc.at[2 + i]) for i, ref in enumerate((first, second))
    ]
    for copy in own_moments:
        copy.start()
    def place(h, k):
        return MM.at[pl.ds(pl.multiple_of((z * 4 + h * 2 + k) * CAP, CAP), CAP)]

    targets = ((twin, xl, 1 - c), (across, 1 - xl, c), (diagonal, 1 - xl, 1 - c))

    def moments_to(i):
        to, h, k = targets[i]
        return remote(MT.at[i], place(xl, c), tws.at[1 + i], twr.at[1 + i], to)

    for i, copy in enumerate(own_moments):
        copy.wait()
        place(xl, c)[:, i] = MO[i, c, 0, :, :, columns].astype(BF16)
        MT[0, :, i] = MO[i, 1 - c, 0, :, :, columns].astype(BF16)
        MT[1, :, i] = MO[i, c, 0, :, :, others].astype(BF16)
        MT[2, :, i] = MO[i, 1 - c, 0, :, :, others].astype(BF16)
    own_raw.wait()
    pl.semaphore_wait(barrier, len(partners))

    for i in range(3):
        y_send(i).start()
    t_grads = remote(grads.at[0, 1 - c], T, tws.at[0], twr.at[0], twin)
    t_grads.start()
    for i in range(3):
        moments_to(i).start()
    own_grads.wait()
    t_grads.wait_recv()
    r_start()
    for i, (to, h, k) in enumerate(targets):
        remote(MT.at[i], place(h, k), tws.at[1 + i], twr.at[1 + i], to).wait_recv()
    m_start()

    y_recv(2)
    y_send(3).start()
    y_send(4).start()

    def gram(h, yy):
        part = fblock(h, yy)[...]
        return mm(part, part, 0, 0)

    A[...] = gram(xh, y) + gram(1 - xh, y)
    y_recv(0)
    y_send(5).start()
    y_recv(1)
    y_send(6).start()
    A[...] = A[...] + (gram(xh, y - 1) + gram(xh, y + 1))
    r_step(1)
    y_recv(3)
    y_send(7).start()
    y_recv(4)
    y_send(8).start()
    A[...] = A[...] + (gram(1 - xh, y - 1) + gram(1 - xh, y + 1))
    m_step(1)
    for i in range(5, 9):
        y_recv(i)
    A[...] = A[...] + (gram(xh, y + 2) + gram(1 - xh, y + 2))
    for i in range(9):
        y_send(i).wait_send()

    hooks = {
        0: {2: lambda: r_step(2), 6: lambda: m_step(2)},
        1: {2: lambda: r_step(3), 6: lambda: m_step(3)},
        2: {5: r_last},
        3: {2: lambda: m_step(4), 6: r_sum},
    }
    factor(A, X, S, Q, hooks)
    g_start()

    for lo in range(0, Q.shape[1], BLK):
        QT[lo : lo + BLK, :] = Q[:, lo : lo + BLK].T

    def rows_of(k):
        return pl.ds(pl.multiple_of(zat(k) * 128, 128), 128)

    def u_across(i, k, part):
        there = U.at[rows_of(k), part]
        return remote(there, there, us.at[i], ur.at[i], across)

    def d_own(i, k):
        return pltpu.make_async_copy(D.at[rows_of(k), :], delta_out.at[c, rows_of(k), :], do.at[i])

    def d_twin(i, k, at):
        return remote(D.at[rows_of(k), :], delta_out.at[at, rows_of(k), :], ds.at[i], dr.at[i], twin)

    def update(i, k):
        @pl.loop(0, 8)
        def _(j):
            b = zat(k) * 8 + j
            moments = MM[slots[c, b]]
            U[pl.ds(pl.multiple_of(b * ROWS, ROWS), ROWS), columns] = scaled_update(
                moments[0].astype(F32), moments[1].astype(F32), PB[b].astype(F32)
            )

        u_across(i, k, columns).start()

    def delta(i, k):
        u_across(i, k, others).wait_recv()
        D[rows_of(k), :] = mm(U[rows_of(k), :], QT[...], 1, 0, None).astype(BF16)
        d_own(i, k).start()
        d_twin(i, k, c).start()

    order = (0, -1, 1, -2, 2, -3, 3, 4)
    update(0, 0)
    for s in range(1, 4):
        g_step(s)
        update(2 * s - 1, -s)
        update(2 * s, s)
        for i in range(max(2 * s - 3, 0), 2 * s - 1):
            delta(i, order[i])
    g_step(4)
    update(7, 4)

    holders = ((xl, c), (xl, 1 - c), (1 - xl, c), (1 - xl, 1 - c))
    to_holders = (None, twin, across, diagonal)

    def rows_to(n, matrix, part):
        return remote(GT.at[n], rows_out.at[matrix, :, :, part], es.at[n - 1], er.at[n - 1], to_holders[n])

    for n, (h, k) in enumerate(holders):
        for i in range(CAP):
            GT[n, i] = PB[bucket_of[c, (z * 4 + h * 2 + k) * CAP + i]]
    r_own = pltpu.make_async_copy(GT.at[0], rows_out.at[c, :, :, columns], loc.at[4])
    r_own.start()
    for n in range(1, 4):
        rows_to(n, c, columns).start()
    for i in range(5, 8):
        delta(i, order[i])

    for i, k in enumerate(order):
        d_own(i, k).wait()
        d_twin(i, k, c).wait_send()
        u_across(i, k, columns).wait_send()
    for i, k in enumerate(order):
        d_twin(i, -k, 1 - c).wait_recv()
    r_own.wait()
    for n in range(1, 4):
        rows_to(n, c, columns).wait_send()
    rows_to(1, 1 - c, columns).wait_recv()
    rows_to(2, c, others).wait_recv()
    rows_to(3, 1 - c, others).wait_recv()
    t_grads.wait_send()
    for i in range(3):
        moments_to(i).wait_send()
    for s in range(4):
        ra(s).wait_send()
        mz(s, 1, -s).wait_send()
        gz(s, 1, -s).wait_send()
    for s in range(3):
        rb(s).wait_send()
        mz(s, -1, s).wait_send()
        gz(s, -1, s).wait_send()


def shards(grads, raw_proj, bucket_owner, first_moment, second_moment):
    matrices, local_rows, features = grads.shape[1:]
    rank = raw_proj.shape[2]
    buckets = bucket_owner.shape[1]
    capacity = first_moment.shape[2]
    slot_total = lax.axis_size("dp") * capacity
    same = bucket_owner[:, :, None] == bucket_owner[:, None, :]
    earlier = jnp.arange(buckets)[None, :] < jnp.arange(buckets)[:, None]
    ranks = jnp.sum(jnp.logical_and(same, earlier).astype(jnp.int32), axis=-1)
    slots = bucket_owner * capacity + ranks
    matches = slots[:, None, :] == jnp.arange(slot_total, dtype=jnp.int32)[None, :, None]
    occupied = jnp.any(matches, axis=2)
    bucket_of = jnp.sum(
        matches.astype(jnp.int32) * jnp.arange(buckets, dtype=jnp.int32)[None, None, :], axis=2
    )
    smem = pl.BlockSpec(memory_space=pltpu.SMEM)
    anywhere = pl.BlockSpec(memory_space=pl.ANY)
    piece = (local_rows // NZ, features)
    dma = pltpu.SemaphoreType.DMA
    weight_delta, grad_rows = pl.pallas_call(
        kernel,
        out_shape=(
            jax.ShapeDtypeStruct((matrices, local_rows, features), BF16),
            jax.ShapeDtypeStruct((matrices, capacity, ROWS, rank), BF16),
        ),
        in_specs=[smem, smem] + [anywhere] * 4,
        out_specs=(anywhere, anywhere),
        scratch_shapes=[
            pltpu.VMEM((features, rank), F32),
            pltpu.VMEM((rank, rank), F32),
            pltpu.VMEM((BLK, 2 * BLK), F32),
            pltpu.VMEM((features, rank), BF16),
            pltpu.VMEM((rank, features), BF16),
            pltpu.VMEM((local_rows, features), BF16),
            pltpu.VMEM((local_rows, features), BF16),
            pltpu.VMEM((4, *piece), BF16),
            pltpu.VMEM((3, *piece), BF16),
            pltpu.VMEM(piece, BF16),
            pltpu.VMEM(piece, BF16),
            pltpu.VMEM(piece, BF16),
            pltpu.VMEM(piece, BF16),
            pltpu.VMEM((slot_total, 2, ROWS, rank // 2), BF16),
            pltpu.VMEM((2, *first_moment.shape), F32),
            pltpu.VMEM((buckets, ROWS, rank // 2), BF16),
            pltpu.VMEM((local_rows, rank), BF16),
            pltpu.VMEM((local_rows, features), BF16),
            pltpu.VMEM((4, capacity, ROWS, rank // 2), BF16),
            pltpu.VMEM((3, capacity, 2, ROWS, rank // 2), BF16),
            dma((5,)), dma((8,)), dma((8,)), dma((8,)), dma((8,)), dma((8,)),
            dma((9,)), dma((9,)), dma((4,)), dma((4,)), dma((7,)), dma((7,)),
            dma((7,)), dma((7,)), dma, dma, dma((7,)), dma((7,)), dma((3,)), dma((3,)),
        ],
        compiler_params=pltpu.CompilerParams(
            collective_id=0, has_side_effects=True, vmem_limit_bytes=56 << 20
        ),
        cost_estimate=pl.CostEstimate(
            flops=10_000_000_000, bytes_accessed=16_000_000, transcendentals=1_000_000
        ),
    )(slots, bucket_of, grads, raw_proj, first_moment, second_moment)
    start = lax.axis_index("dp") * capacity
    keep = lax.dynamic_slice_in_dim(occupied, start, capacity, 1)[:, :, None, None]
    first, second = first_moment[:, 0], second_moment[:, 0]
    grad_rows = grad_rows.astype(F32)
    first_out = jnp.where(keep, 0.9 * first + 0.1 * grad_rows, first)[:, None]
    second_out = jnp.where(keep, 0.999 * second + 0.001 * grad_rows * grad_rows, second)[:, None]
    return (weight_delta, first_out, second_out)


def solution(mesh):
    return jax.shard_map(
        shards,
        mesh=mesh,
        in_specs=(
            P("dp", None, "fsdp", None),
            P(None, "fsdp", None),
            P(None, "fsdp"),
            P(None, "fsdp", "dp", None, None),
            P(None, "fsdp", "dp", None, None),
        ),
        out_specs=(
            P(None, "fsdp", None),
            P(None, "fsdp", "dp", None, None),
            P(None, "fsdp", "dp", None, None),
        ),
        check_vma=False,
    )
```

```python
import jax
import jax.numpy as jnp
from jax import lax
from jax.experimental import pallas as pl
from jax.experimental.pallas import tpu as pltpu
from jax.sharding import PartitionSpec as P

HI = lax.Precision.HIGHEST
F32 = jnp.float32
BF16 = jnp.bfloat16
BLK = 128
PAN = 16
NZ, NY, CAP, ROWS = 8, 4, 4, 16


def mm(a, b, ca, cb, precision=HI):
    return lax.dot_general(
        a, b, (((ca,), (cb,)), ((), ())), precision=precision, preferred_element_type=F32
    )


def split(x):
    high = x.astype(BF16).astype(F32)
    middle = (x - high).astype(BF16).astype(F32)
    return high, middle, (x - high) - middle


def mm3(a, b, ca, cb):
    ah, bh = a.astype(BF16), b.astype(BF16)
    al, bl = (a - ah.astype(F32)).astype(BF16), (b - bh.astype(F32)).astype(BF16)
    return mm(ah, bh, ca, cb, None) + (mm(ah, bl, ca, cb, None) + mm(al, bh, ca, cb, None))


def panel(S, g):
    rows = pl.ds(pl.multiple_of(PAN * g, PAN), PAN)
    V, W = S[rows, 0:BLK], S[rows, BLK : 2 * BLK]
    turned = pltpu.roll(V, lax.rem(BLK - PAN * g, BLK), 1)
    C = [jnp.broadcast_to(turned[:, k : k + 1], (PAN, BLK)) for k in range(PAN)]
    sub = lax.broadcasted_iota(jnp.int32, (PAN, BLK), 0)
    lane = lax.broadcasted_iota(jnp.int32, (PAN, BLK), 1)
    pivot = jnp.ones((PAN, BLK), F32)
    for j in range(PAN):
        p = C[j][j : j + 1, :]
        pivot = jnp.where(sub == j, jnp.broadcast_to(p, (PAN, BLK)), pivot)
        if j < PAN - 1:
            m = jnp.where(sub > j, C[j] * jnp.broadcast_to(1.0 / p, (PAN, BLK)), 0.0)
            for k in range(j + 1, PAN):
                C[k] = C[k] - m * jnp.broadcast_to(C[k][j : j + 1, :], (PAN, BLK))
            V = V - m * jnp.broadcast_to(V[j : j + 1, :], (PAN, BLK))
            W = W - m * jnp.broadcast_to(W[j : j + 1, :], (PAN, BLK))
    s = lax.rsqrt(pivot)
    s = s * (1.5 - 0.5 * pivot * s * s)
    VW = jnp.concatenate([V * s, W * s], axis=1)
    S[rows, :] = VW
    high, middle, low = split(VW)
    h, m, l = (jnp.where(lane >= PAN * (g + 1), x[:, 0:BLK], 0.0) for x in (high, middle, low))
    left = jnp.concatenate([h, h, m, h, l, m], axis=0).astype(BF16)
    right = jnp.concatenate([high, middle, high, low, high, middle], axis=0).astype(BF16)
    S[...] = S[...] - mm(left, right, 0, 0, None)


def factor(A, X, S, Q, hooks):
    eye = (
        lax.broadcasted_iota(jnp.int32, (BLK, BLK), 0)
        == lax.broadcasted_iota(jnp.int32, (BLK, BLK), 1)
    ).astype(F32)
    blocks = A.shape[0] // BLK
    for k in range(blocks):
        lo, hi = BLK * k, BLK * k + BLK
        S[:, 0:BLK] = A[lo:hi, lo:hi]
        S[:, BLK : 2 * BLK] = eye

        @pl.loop(0, BLK // PAN)
        def _(g):
            panel(S, g)
            for at, hook in hooks.get(k, {}).items():
                pl.when(g == at)(hook)

        inverse = S[:, BLK : 2 * BLK]
        q = mm3(X[:, lo:hi], inverse, 1, 1)
        Q[:, lo:hi] = q.astype(BF16)
        if k < blocks - 1:
            U = mm(inverse, A[lo:hi, hi:], 1, 0)
            A[hi:, hi:] = A[hi:, hi:] - mm(U, U, 0, 0)
            X[:, hi:] = X[:, hi:] - mm3(q, U, 1, 0)


def scaled_update(first, second, g):
    new_first = 0.9 * first + 0.1 * g
    new_second = 0.999 * second + 0.001 * g * g
    scaled = 6.0 * (new_first / (1.0 - 0.9**10)) / (jnp.sqrt(new_second / (1.0 - 0.999**10)) + 1e-08)
    return scaled.astype(BF16)


def kernel(
    slots, bucket_of, grads, raw, first, second, delta_out, rows_out,
    X, A, S, Q, QT, G, T, RA, RB, SA, SB, XS, XR, GS, MM, MO, PB, U, GT, MT,
    loc, ds, dr, us, ur, ys, yr, tws, twr, mzs, mzr, rs, rr, xs, xr, gs, gr, es, er,
):
    dp, f = lax.axis_index("dp"), lax.axis_index("fsdp")
    z, xl, c = dp // 4, lax.rem(dp // 2, 2), lax.rem(dp, 2)
    xh, y = f // NY, lax.rem(f, NY)
    d = 1 - 2 * c

    def zat(k):
        return lax.rem(z + d * k + 2 * NZ, NZ)

    def at_z(k):
        return (zat(k) * 4 + xl * 2 + c, f)

    ahead, behind = at_z(1), at_z(-1)
    across = (z * 4 + (1 - xl) * 2 + c, f)
    twin = (z * 4 + xl * 2 + 1 - c, f)
    diagonal = (z * 4 + (1 - xl) * 2 + 1 - c, f)
    half = Q.shape[1] // 2
    columns = pl.ds(pl.multiple_of(xl * half, half), half)
    others = pl.ds(pl.multiple_of((1 - xl) * half, half), half)
    up, down = (dp, xh * NY + lax.rem(y + 1, NY)), (dp, xh * NY + lax.rem(y + NY - 1, NY))
    mirror = (z * 4 + (1 - xl) * 2 + c, (1 - xh) * NY + y)

    def remote(src, dst, send, recv, to):
        return pltpu.make_async_remote_copy(
            src_ref=src, dst_ref=dst, send_sem=send, recv_sem=recv,
            device_id=to, device_id_type=pl.DeviceIdType.MESH,
        )

    def fblock(h, yy, lo=0, n=128):
        return X.at[pl.ds(pl.multiple_of((h * NY + lax.rem(yy + 2 * NY, NY)) * 128 + lo, 64), n), :]

    def y_send(i):
        what = [
            (fblock(xh, y), up), (fblock(xh, y), down), (fblock(xh, y), mirror),
            (fblock(1 - xh, y), up), (fblock(1 - xh, y), down),
            (fblock(xh, y - 1, 0, 64), up), (fblock(xh, y + 1, 64, 64), down),
            (fblock(1 - xh, y - 1, 0, 64), up), (fblock(1 - xh, y + 1, 64, 64), down),
        ][i]
        return remote(what[0], what[0], ys.at[i], yr.at[i], what[1])

    def y_recv(i):
        what = [
            fblock(xh, y - 1), fblock(xh, y + 1), fblock(1 - xh, y),
            fblock(1 - xh, y - 1), fblock(1 - xh, y + 1),
            fblock(xh, y - 2, 0, 64), fblock(xh, y + 2, 64, 64),
            fblock(1 - xh, y - 2, 0, 64), fblock(1 - xh, y + 2, 64, 64),
        ][i]
        remote(what, what, ys.at[i], yr.at[i], up).wait_recv()

    def mblock(k):
        return MM.at[pl.ds(pl.multiple_of(zat(k) * 16, 16), 16)]

    def mz(s, way, k):
        i = s if way > 0 else 4 + s
        return remote(mblock(k), mblock(k), mzs.at[i], mzr.at[i], ahead if way > 0 else behind)

    def m_start():
        mz(0, 1, 0).start()
        mz(0, -1, 0).start()

    def m_step(s):
        mz(s - 1, 1, -s).wait_recv()
        if s < 4:
            mz(s, 1, -s).start()
            mz(s - 1, -1, s).wait_recv()
            if s < 3:
                mz(s, -1, s).start()

    pieces = (4, -3, 3, -2, 2, -1, 1, 0)

    def two_cores(k, h):
        rows = pl.ds(pl.multiple_of(zat(k) * 128 + h * 64, 64), 64)
        return G[rows, :].astype(F32) + T[rows, :].astype(F32)

    def x_piece(i):
        return remote(XS.at[i], XR.at[i], xs.at[i], xr.at[i], across)

    def x_start():
        for i, k in enumerate(pieces):
            XS[i] = two_cores(k, 1 - xl).astype(BF16)
            x_piece(i).start()

    def own(k):
        i = pieces.index(k)
        x_piece(i).wait_recv()
        return two_cores(k, xl) + XR[i].astype(F32)

    def ra(s):
        return remote(SA if s == 0 else RA.at[s - 1], RA.at[s], rs.at[s], rr.at[s], ahead)

    def rb(s):
        return remote(SB if s == 0 else RB.at[s - 1], RB.at[s], rs.at[4 + s], rr.at[4 + s], behind)

    def r_start():
        SA[...] = own(4).astype(BF16)
        ra(0).start()
        SB[...] = own(-3).astype(BF16)
        rb(0).start()

    def r_step(s):
        ra(s - 1).wait_recv()
        RA[s - 1] = (RA[s - 1].astype(F32) + own(4 - s)).astype(BF16)
        ra(s).start()
        if s < 3:
            rb(s - 1).wait_recv()
            RB[s - 1] = (RB[s - 1].astype(F32) + own(s - 3)).astype(BF16)
            rb(s).start()

    def half_sum(h):
        there = GS.at[pl.ds(pl.multiple_of(h * 64, 64), 64), :]
        return remote(there, there, xs.at[8], xr.at[8], across)

    def r_last():
        mine = own(0)
        ra(3).wait_recv()
        rb(2).wait_recv()
        GS[pl.ds(pl.multiple_of(xl * 64, 64), 64), :] = (
            mine + (RA[3].astype(F32) + RB[2].astype(F32))
        ).astype(BF16)
        half_sum(xl).start()

    def r_sum():
        half_sum(1 - xl).wait_recv()

    def pblock(k):
        return PB.at[pl.ds(pl.multiple_of(zat(k) * 8, 8), 8)]

    def gz(s, way, k):
        i = s if way > 0 else 4 + s
        return remote(pblock(k), pblock(k), gs.at[i], gr.at[i], ahead if way > 0 else behind)

    def g_start():
        part = mm(GS[...], Q[:, columns], 1, 0, None)
        pblock(0)[...] = part.reshape(8, ROWS, part.shape[1]).astype(BF16)
        gz(0, 1, 0).start()
        gz(0, -1, 0).start()

    def g_step(s):
        gz(s - 1, 1, -s).wait_recv()
        if s < 4:
            gz(s, 1, -s).start()
            gz(s - 1, -1, s).wait_recv()
            if s < 3:
                gz(s, -1, s).start()

    partners = (ahead, behind, across, twin, diagonal, up, down, mirror)
    barrier = pltpu.get_barrier_semaphore()
    for to in partners:
        pl.semaphore_signal(barrier, inc=1, device_id=to, device_id_type=pl.DeviceIdType.MESH)
    own_raw = pltpu.make_async_copy(raw.at[c], fblock(xh, y), loc.at[0])
    own_grads = pltpu.make_async_copy(grads.at[0, c], G, loc.at[1])
    own_raw.start()
    own_grads.start()
    own_moments = [
        pltpu.make_async_copy(ref, MO.at[i], loc.at[2 + i]) for i, ref in enumerate((first, second))
    ]
    for copy in own_moments:
        copy.start()
    def place(h, k):
        return MM.at[pl.ds(pl.multiple_of((z * 4 + h * 2 + k) * CAP, CAP), CAP)]

    targets = ((twin, xl, 1 - c), (across, 1 - xl, c), (diagonal, 1 - xl, 1 - c))

    def moments_to(i):
        to, h, k = targets[i]
        return remote(MT.at[i], place(xl, c), tws.at[1 + i], twr.at[1 + i], to)

    for i, copy in enumerate(own_moments):
        copy.wait()
        place(xl, c)[:, i] = MO[i, c, 0, :, :, columns].astype(BF16)
        MT[0, :, i] = MO[i, 1 - c, 0, :, :, columns].astype(BF16)
        MT[1, :, i] = MO[i, c, 0, :, :, others].astype(BF16)
        MT[2, :, i] = MO[i, 1 - c, 0, :, :, others].astype(BF16)
    own_raw.wait()
    pl.semaphore_wait(barrier, len(partners))

    for i in range(3):
        y_send(i).start()
    t_grads = remote(grads.at[0, 1 - c], T, tws.at[0], twr.at[0], twin)
    t_grads.start()
    for i in range(3):
        moments_to(i).start()
    own_grads.wait()
    t_grads.wait_recv()
    x_start()
    for i, (to, h, k) in enumerate(targets):
        remote(MT.at[i], place(h, k), tws.at[1 + i], twr.at[1 + i], to).wait_recv()
    m_start()

    y_recv(2)
    y_send(3).start()
    y_send(4).start()

    def gram(h, yy):
        part = fblock(h, yy)[...]
        return mm(part, part, 0, 0)

    A[...] = gram(xh, y) + gram(1 - xh, y)
    r_start()
    y_recv(0)
    y_send(5).start()
    y_recv(1)
    y_send(6).start()
    A[...] = A[...] + (gram(xh, y - 1) + gram(xh, y + 1))
    y_recv(3)
    y_send(7).start()
    y_recv(4)
    y_send(8).start()
    A[...] = A[...] + (gram(1 - xh, y - 1) + gram(1 - xh, y + 1))
    m_step(1)
    for i in range(5, 9):
        y_recv(i)
    A[...] = A[...] + (gram(xh, y + 2) + gram(1 - xh, y + 2))
    for i in range(9):
        y_send(i).wait_send()

    hooks = {
        0: {0: lambda: r_step(1), 4: lambda: m_step(2), 7: lambda: r_step(2)},
        1: {3: lambda: m_step(3), 6: lambda: r_step(3)},
        2: {3: r_last, 6: lambda: m_step(4)},
        3: {4: r_sum},
    }
    factor(A, X, S, Q, hooks)
    g_start()

    for lo in range(0, Q.shape[1], BLK):
        QT[lo : lo + BLK, :] = Q[:, lo : lo + BLK].T

    def rows_of(k):
        return pl.ds(pl.multiple_of(zat(k) * 128, 128), 128)

    def u_across(i, k, part):
        there = U.at[rows_of(k), part]
        return remote(there, there, us.at[i], ur.at[i], across)

    def d_twin(i, k, at):
        there = delta_out.at[at, rows_of(k), :]
        return remote(there, there, ds.at[i], dr.at[i], twin)

    def update(i, k):
        @pl.loop(0, 8)
        def _(j):
            b = zat(k) * 8 + j
            moments = MM[slots[c, b]]
            U[pl.ds(pl.multiple_of(b * ROWS, ROWS), ROWS), columns] = scaled_update(
                moments[0].astype(F32), moments[1].astype(F32), PB[b].astype(F32)
            )

        u_across(i, k, columns).start()

    def delta(i, k):
        u_across(i, k, others).wait_recv()
        delta_out[c, rows_of(k), :] = mm(U[rows_of(k), :], QT[...], 1, 0, None).astype(BF16)
        d_twin(i, k, c).start()

    order = (0, -1, 1, -2, 2, -3, 3, 4)
    update(0, 0)
    for s in range(1, 4):
        g_step(s)
        update(2 * s - 1, -s)
        update(2 * s, s)
        for i in range(max(2 * s - 3, 0), 2 * s - 1):
            delta(i, order[i])
    g_step(4)
    update(7, 4)

    holders = ((xl, c), (xl, 1 - c), (1 - xl, c), (1 - xl, 1 - c))
    to_holders = (None, twin, across, diagonal)

    def rows_to(n, matrix, part):
        return remote(GT.at[n], rows_out.at[matrix, :, :, part], es.at[n - 1], er.at[n - 1], to_holders[n])

    for n, (h, k) in enumerate(holders):
        for i in range(CAP):
            GT[n, i] = PB[bucket_of[c, (z * 4 + h * 2 + k) * CAP + i]]
    r_own = pltpu.make_async_copy(GT.at[0], rows_out.at[c, :, :, columns], loc.at[4])
    r_own.start()
    for n in range(1, 4):
        rows_to(n, c, columns).start()
    for i in range(5, 8):
        delta(i, order[i])

    for i, k in enumerate(order):
        d_twin(i, k, c).wait_send()
        u_across(i, k, columns).wait_send()
    for i, k in enumerate(order):
        d_twin(i, -k, 1 - c).wait_recv()
    r_own.wait()
    for n in range(1, 4):
        rows_to(n, c, columns).wait_send()
    rows_to(1, 1 - c, columns).wait_recv()
    rows_to(2, c, others).wait_recv()
    rows_to(3, 1 - c, others).wait_recv()
    t_grads.wait_send()
    half_sum(xl).wait_send()
    for i in range(8):
        x_piece(i).wait_send()
    for i in range(3):
        moments_to(i).wait_send()
    for s in range(4):
        ra(s).wait_send()
        mz(s, 1, -s).wait_send()
        gz(s, 1, -s).wait_send()
    for s in range(3):
        rb(s).wait_send()
        mz(s, -1, s).wait_send()
        gz(s, -1, s).wait_send()


def shards(grads, raw_proj, bucket_owner, first_moment, second_moment):
    matrices, local_rows, features = grads.shape[1:]
    rank = raw_proj.shape[2]
    buckets = bucket_owner.shape[1]
    capacity = first_moment.shape[2]
    slot_total = lax.axis_size("dp") * capacity
    same = bucket_owner[:, :, None] == bucket_owner[:, None, :]
    earlier = jnp.arange(buckets)[None, :] < jnp.arange(buckets)[:, None]
    ranks = jnp.sum(jnp.logical_and(same, earlier).astype(jnp.int32), axis=-1)
    slots = bucket_owner * capacity + ranks
    matches = slots[:, None, :] == jnp.arange(slot_total, dtype=jnp.int32)[None, :, None]
    occupied = jnp.any(matches, axis=2)
    bucket_of = jnp.sum(
        matches.astype(jnp.int32) * jnp.arange(buckets, dtype=jnp.int32)[None, None, :], axis=2
    )
    smem = pl.BlockSpec(memory_space=pltpu.SMEM)
    anywhere = pl.BlockSpec(memory_space=pl.ANY)
    piece = (local_rows // NZ // 2, features)
    dma = pltpu.SemaphoreType.DMA
    weight_delta, grad_rows = pl.pallas_call(
        kernel,
        out_shape=(
            pltpu.VMEM((matrices, local_rows, features), BF16),
            jax.ShapeDtypeStruct((matrices, capacity, ROWS, rank), BF16),
        ),
        in_specs=[smem, smem] + [anywhere] * 4,
        out_specs=(pl.BlockSpec(memory_space=pltpu.VMEM), anywhere),
        scratch_shapes=[
            pltpu.VMEM((features, rank), F32),
            pltpu.VMEM((rank, rank), F32),
            pltpu.VMEM((BLK, 2 * BLK), F32),
            pltpu.VMEM((features, rank), BF16),
            pltpu.VMEM((rank, features), BF16),
            pltpu.VMEM((local_rows, features), BF16),
            pltpu.VMEM((local_rows, features), BF16),
            pltpu.VMEM((4, *piece), BF16),
            pltpu.VMEM((3, *piece), BF16),
            pltpu.VMEM(piece, BF16),
            pltpu.VMEM(piece, BF16),
            pltpu.VMEM((8, *piece), BF16),
            pltpu.VMEM((8, *piece), BF16),
            pltpu.VMEM((local_rows // NZ, features), BF16),
            pltpu.VMEM((slot_total, 2, ROWS, rank // 2), BF16),
            pltpu.VMEM((2, *first_moment.shape), F32),
            pltpu.VMEM((buckets, ROWS, rank // 2), BF16),
            pltpu.VMEM((local_rows, rank), BF16),
            pltpu.VMEM((4, capacity, ROWS, rank // 2), BF16),
            pltpu.VMEM((3, capacity, 2, ROWS, rank // 2), BF16),
            dma((5,)), dma((8,)), dma((8,)), dma((8,)), dma((8,)),
            dma((9,)), dma((9,)), dma((4,)), dma((4,)), dma((7,)), dma((7,)),
            dma((7,)), dma((7,)), dma((9,)), dma((9,)), dma((7,)), dma((7,)), dma((3,)), dma((3,)),
        ],
        compiler_params=pltpu.CompilerParams(
            collective_id=0, has_side_effects=True, vmem_limit_bytes=56 << 20
        ),
        cost_estimate=pl.CostEstimate(
            flops=10_000_000_000, bytes_accessed=16_000_000, transcendentals=1_000_000
        ),
    )(slots, bucket_of, grads, raw_proj, first_moment, second_moment)
    start = lax.axis_index("dp") * capacity
    keep = lax.dynamic_slice_in_dim(occupied, start, capacity, 1)[:, :, None, None]
    first, second = first_moment[:, 0], second_moment[:, 0]
    grad_rows = grad_rows.astype(F32)
    first_out = jnp.where(keep, 0.9 * first + 0.1 * grad_rows, first)[:, None]
    second_out = jnp.where(keep, 0.999 * second + 0.001 * grad_rows * grad_rows, second)[:, None]
    return (weight_delta, first_out, second_out)


def solution(mesh):
    return jax.shard_map(
        shards,
        mesh=mesh,
        in_specs=(
            P("dp", None, "fsdp", None),
            P(None, "fsdp", None),
            P(None, "fsdp"),
            P(None, "fsdp", "dp", None, None),
            P(None, "fsdp", "dp", None, None),
        ),
        out_specs=(
            P(None, "fsdp", None),
            P(None, "fsdp", "dp", None, None),
            P(None, "fsdp", "dp", None, None),
        ),
        check_vma=False,
    )
```

```python
import jax
import jax.numpy as jnp
from jax import lax
from jax.experimental import pallas as pl
from jax.experimental.pallas import tpu as pltpu
from jax.sharding import PartitionSpec as P

HI = lax.Precision.HIGHEST
F32 = jnp.float32
BF16 = jnp.bfloat16
BLK = 128
PAN = 16
NZ, NY, CAP, ROWS = 8, 4, 4, 16


def mm(a, b, ca, cb, precision=HI):
    return lax.dot_general(
        a, b, (((ca,), (cb,)), ((), ())), precision=precision, preferred_element_type=F32
    )


def split(x):
    high = x.astype(BF16).astype(F32)
    middle = (x - high).astype(BF16).astype(F32)
    return high, middle, (x - high) - middle


def mm3(a, b, ca, cb):
    ah, bh = a.astype(BF16), b.astype(BF16)
    al, bl = (a - ah.astype(F32)).astype(BF16), (b - bh.astype(F32)).astype(BF16)
    return mm(ah, bh, ca, cb, None) + (mm(ah, bl, ca, cb, None) + mm(al, bh, ca, cb, None))


def panel(S, g):
    rows = pl.ds(pl.multiple_of(PAN * g, PAN), PAN)
    V, W = S[rows, 0:BLK], S[rows, BLK : 2 * BLK]
    turned = pltpu.roll(V, lax.rem(BLK - PAN * g, BLK), 1)
    C = [jnp.broadcast_to(turned[:, k : k + 1], (PAN, BLK)) for k in range(PAN)]
    sub = lax.broadcasted_iota(jnp.int32, (PAN, BLK), 0)
    lane = lax.broadcasted_iota(jnp.int32, (PAN, BLK), 1)
    pivot = jnp.ones((PAN, BLK), F32)
    for j in range(PAN):
        p = C[j][j : j + 1, :]
        pivot = jnp.where(sub == j, jnp.broadcast_to(p, (PAN, BLK)), pivot)
        if j < PAN - 1:
            m = jnp.where(sub > j, C[j] * jnp.broadcast_to(1.0 / p, (PAN, BLK)), 0.0)
            for k in range(j + 1, PAN):
                C[k] = C[k] - m * jnp.broadcast_to(C[k][j : j + 1, :], (PAN, BLK))
            V = V - m * jnp.broadcast_to(V[j : j + 1, :], (PAN, BLK))
            W = W - m * jnp.broadcast_to(W[j : j + 1, :], (PAN, BLK))
    s = lax.rsqrt(pivot)
    s = s * (1.5 - 0.5 * pivot * s * s)
    VW = jnp.concatenate([V * s, W * s], axis=1)
    S[rows, :] = VW
    high, middle, low = split(VW)
    h, m, l = (jnp.where(lane >= PAN * (g + 1), x[:, 0:BLK], 0.0) for x in (high, middle, low))
    left = jnp.concatenate([h, h, m, h, l, m], axis=0).astype(BF16)
    right = jnp.concatenate([high, middle, high, low, high, middle], axis=0).astype(BF16)
    S[...] = S[...] - mm(left, right, 0, 0, None)


def factor(A, X, S, Q, hooks):
    eye = (
        lax.broadcasted_iota(jnp.int32, (BLK, BLK), 0)
        == lax.broadcasted_iota(jnp.int32, (BLK, BLK), 1)
    ).astype(F32)
    blocks = A.shape[0] // BLK
    for k in range(blocks):
        lo, hi = BLK * k, BLK * k + BLK
        S[:, 0:BLK] = A[lo:hi, lo:hi]
        S[:, BLK : 2 * BLK] = eye

        @pl.loop(0, BLK // PAN)
        def _(g):
            panel(S, g)
            for at, hook in hooks.get(k, {}).items():
                pl.when(g == at)(hook)

        inverse = S[:, BLK : 2 * BLK]
        q = mm3(X[:, lo:hi], inverse, 1, 1)
        Q[:, lo:hi] = q.astype(BF16)
        if k < blocks - 1:
            U = mm(inverse, A[lo:hi, hi:], 1, 0)
            for at in range(hi, A.shape[0], BLK):
                u = U[:, at - hi :]
                A[at : at + BLK, at:] = A[at : at + BLK, at:] - mm(u[:, 0:BLK], u, 0, 0)
            X[:, hi:] = X[:, hi:] - mm3(q, U, 1, 0)


def scaled_update(first, second, g):
    new_first = 0.9 * first + 0.1 * g
    new_second = 0.999 * second + 0.001 * g * g
    scaled = 6.0 * (new_first / (1.0 - 0.9**10)) / (jnp.sqrt(new_second / (1.0 - 0.999**10)) + 1e-08)
    return scaled.astype(BF16)


def kernel(
    slots, bucket_of, grads, raw, first, second, delta_out, rows_out,
    X, A, S, Q, QT, G, T, RA, RB, SA, SB, XS, XR, GS, MM, MO, PB, U, GT, MT,
    loc, ds, dr, us, ur, ys, yr, tws, twr, mzs, mzr, rs, rr, xs, xr, gs, gr, es, er,
):
    dp, f = lax.axis_index("dp"), lax.axis_index("fsdp")
    z, xl, c = dp // 4, lax.rem(dp // 2, 2), lax.rem(dp, 2)
    xh, y = f // NY, lax.rem(f, NY)
    d = 1 - 2 * c

    def zat(k):
        return lax.rem(z + d * k + 2 * NZ, NZ)

    def at_z(k):
        return (zat(k) * 4 + xl * 2 + c, f)

    ahead, behind = at_z(1), at_z(-1)
    across = (z * 4 + (1 - xl) * 2 + c, f)
    twin = (z * 4 + xl * 2 + 1 - c, f)
    diagonal = (z * 4 + (1 - xl) * 2 + 1 - c, f)
    half = Q.shape[1] // 2
    columns = pl.ds(pl.multiple_of(xl * half, half), half)
    others = pl.ds(pl.multiple_of((1 - xl) * half, half), half)
    up, down = (dp, xh * NY + lax.rem(y + 1, NY)), (dp, xh * NY + lax.rem(y + NY - 1, NY))
    mirror = (z * 4 + (1 - xl) * 2 + c, (1 - xh) * NY + y)

    def remote(src, dst, send, recv, to):
        return pltpu.make_async_remote_copy(
            src_ref=src, dst_ref=dst, send_sem=send, recv_sem=recv,
            device_id=to, device_id_type=pl.DeviceIdType.MESH,
        )

    def fblock(h, yy, lo=0, n=128):
        return X.at[pl.ds(pl.multiple_of((h * NY + lax.rem(yy + 2 * NY, NY)) * 128 + lo, 64), n), :]

    def y_send(i):
        what = [
            (fblock(xh, y), up), (fblock(xh, y), down), (fblock(xh, y), mirror),
            (fblock(1 - xh, y, 64, 64), up), (fblock(1 - xh, y, 64, 64), down),
            (fblock(xh, y - 1, 0, 64), up), (fblock(xh, y + 1, 64, 64), down),
            (fblock(1 - xh, y - 1, 0, 64), up), (fblock(1 - xh, y + 1, 64, 64), down),
            (fblock(xh, y - 1, 0, 64), mirror), (fblock(xh, y + 1, 0, 64), mirror),
        ][i]
        return remote(what[0], what[0], ys.at[i], yr.at[i], what[1])

    def y_recv(i):
        what = [
            fblock(xh, y - 1), fblock(xh, y + 1), fblock(1 - xh, y),
            fblock(1 - xh, y - 1, 64, 64), fblock(1 - xh, y + 1, 64, 64),
            fblock(xh, y - 2, 0, 64), fblock(xh, y + 2, 64, 64),
            fblock(1 - xh, y - 2, 0, 64), fblock(1 - xh, y + 2, 64, 64),
            fblock(1 - xh, y - 1, 0, 64), fblock(1 - xh, y + 1, 0, 64),
        ][i]
        remote(what, what, ys.at[i], yr.at[i], up).wait_recv()

    def mblock(k):
        return MM.at[pl.ds(pl.multiple_of(zat(k) * 16, 16), 16)]

    def mz(s, way, k):
        i = s if way > 0 else 4 + s
        return remote(mblock(k), mblock(k), mzs.at[i], mzr.at[i], ahead if way > 0 else behind)

    def m_start():
        mz(0, 1, 0).start()
        mz(0, -1, 0).start()

    def m_step(s):
        mz(s - 1, 1, -s).wait_recv()
        if s < 4:
            mz(s, 1, -s).start()
            mz(s - 1, -1, s).wait_recv()
            if s < 3:
                mz(s, -1, s).start()

    pieces = (4, -3, 3, -2, 2, -1, 1, 0)

    def two_cores(k, h):
        rows = pl.ds(pl.multiple_of(zat(k) * 128 + h * 64, 64), 64)
        return G[rows, :].astype(F32) + T[rows, :].astype(F32)

    def x_piece(i):
        return remote(XS.at[i], XR.at[i], xs.at[i], xr.at[i], across)

    def x_start():
        for i, k in enumerate(pieces):
            XS[i] = two_cores(k, 1 - xl).astype(BF16)
            x_piece(i).start()

    def own(k):
        i = pieces.index(k)
        x_piece(i).wait_recv()
        return two_cores(k, xl) + XR[i].astype(F32)

    def ra(s):
        return remote(SA if s == 0 else RA.at[s - 1], RA.at[s], rs.at[s], rr.at[s], ahead)

    def rb(s):
        return remote(SB if s == 0 else RB.at[s - 1], RB.at[s], rs.at[4 + s], rr.at[4 + s], behind)

    def r_start():
        SA[...] = own(4).astype(BF16)
        ra(0).start()
        SB[...] = own(-3).astype(BF16)
        rb(0).start()

    def r_step(s):
        ra(s - 1).wait_recv()
        RA[s - 1] = (RA[s - 1].astype(F32) + own(4 - s)).astype(BF16)
        ra(s).start()
        if s < 3:
            rb(s - 1).wait_recv()
            RB[s - 1] = (RB[s - 1].astype(F32) + own(s - 3)).astype(BF16)
            rb(s).start()

    def half_sum(h):
        there = GS.at[pl.ds(pl.multiple_of(h * 64, 64), 64), :]
        return remote(there, there, xs.at[8], xr.at[8], across)

    def r_last():
        mine = own(0)
        ra(3).wait_recv()
        rb(2).wait_recv()
        GS[pl.ds(pl.multiple_of(xl * 64, 64), 64), :] = (
            mine + (RA[3].astype(F32) + RB[2].astype(F32))
        ).astype(BF16)
        half_sum(xl).start()

    def r_sum():
        half_sum(1 - xl).wait_recv()

    def pblock(k):
        return PB.at[pl.ds(pl.multiple_of(zat(k) * 8, 8), 8)]

    def gz(s, way, k):
        i = s if way > 0 else 4 + s
        return remote(pblock(k), pblock(k), gs.at[i], gr.at[i], ahead if way > 0 else behind)

    def g_start():
        part = mm(GS[...], Q[:, columns], 1, 0, None)
        pblock(0)[...] = part.reshape(8, ROWS, part.shape[1]).astype(BF16)
        gz(0, 1, 0).start()
        gz(0, -1, 0).start()

    def g_step(s):
        gz(s - 1, 1, -s).wait_recv()
        if s < 4:
            gz(s, 1, -s).start()
            gz(s - 1, -1, s).wait_recv()
            if s < 3:
                gz(s, -1, s).start()

    partners = (ahead, behind, across, twin, diagonal, up, down, mirror)
    barrier = pltpu.get_barrier_semaphore()
    for to in partners:
        pl.semaphore_signal(barrier, inc=1, device_id=to, device_id_type=pl.DeviceIdType.MESH)
    own_raw = pltpu.make_async_copy(raw.at[c], fblock(xh, y), loc.at[0])
    own_grads = pltpu.make_async_copy(grads.at[0, c], G, loc.at[1])
    own_raw.start()
    own_grads.start()
    own_moments = [
        pltpu.make_async_copy(ref, MO.at[i], loc.at[2 + i]) for i, ref in enumerate((first, second))
    ]
    for copy in own_moments:
        copy.start()
    def place(h, k):
        return MM.at[pl.ds(pl.multiple_of((z * 4 + h * 2 + k) * CAP, CAP), CAP)]

    targets = ((twin, xl, 1 - c), (across, 1 - xl, c), (diagonal, 1 - xl, 1 - c))

    def moments_to(i):
        to, h, k = targets[i]
        return remote(MT.at[i], place(xl, c), tws.at[1 + i], twr.at[1 + i], to)

    for i, copy in enumerate(own_moments):
        copy.wait()
        place(xl, c)[:, i] = MO[i, c, 0, :, :, columns].astype(BF16)
        MT[0, :, i] = MO[i, 1 - c, 0, :, :, columns].astype(BF16)
        MT[1, :, i] = MO[i, c, 0, :, :, others].astype(BF16)
        MT[2, :, i] = MO[i, 1 - c, 0, :, :, others].astype(BF16)
    own_raw.wait()
    pl.semaphore_wait(barrier, len(partners))

    for i in range(3):
        y_send(i).start()
    t_grads = remote(grads.at[0, 1 - c], T, tws.at[0], twr.at[0], twin)
    t_grads.start()
    for i in range(3):
        moments_to(i).start()
    own_grads.wait()
    t_grads.wait_recv()
    x_start()
    for i, (to, h, k) in enumerate(targets):
        remote(MT.at[i], place(h, k), tws.at[1 + i], twr.at[1 + i], to).wait_recv()
    m_start()

    def gram(yy, add):
        part = jnp.concatenate([fblock(xh, yy)[...], fblock(1 - xh, yy)[...]], axis=0)
        for lo in range(0, part.shape[1], BLK):
            product = mm(part[:, lo : lo + BLK], part[:, lo:], 0, 0)
            A[lo : lo + BLK, lo:] = A[lo : lo + BLK, lo:] + product if add else product

    for arrived, sends in ((2, (3, 4)), (0, (5, 9)), (1, (6, 10))):
        y_recv(arrived)
        for i in sends:
            y_send(i).start()
    gram(y, False)
    y_recv(4)
    y_send(8).start()
    y_recv(9)
    y_send(7).start()
    r_start()
    y_recv(3)
    gram(y - 1, True)
    y_recv(10)
    gram(y + 1, True)
    m_step(1)
    for i in range(5, 9):
        y_recv(i)
    gram(y + 2, True)
    for i in range(11):
        y_send(i).wait_send()

    hooks = {
        0: {0: lambda: r_step(1), 4: lambda: m_step(2), 7: lambda: r_step(2)},
        1: {3: lambda: m_step(3), 6: lambda: r_step(3)},
        2: {3: r_last, 6: lambda: m_step(4)},
        3: {4: r_sum},
    }
    factor(A, X, S, Q, hooks)
    g_start()

    for lo in range(0, Q.shape[1], BLK):
        QT[lo : lo + BLK, :] = Q[:, lo : lo + BLK].T

    def rows_of(k):
        return pl.ds(pl.multiple_of(zat(k) * 128, 128), 128)

    def u_across(i, k, part):
        there = U.at[rows_of(k), part]
        return remote(there, there, us.at[i], ur.at[i], across)

    def d_twin(i, k, at):
        there = delta_out.at[at, rows_of(k), :]
        return remote(there, there, ds.at[i], dr.at[i], twin)

    def update(i, k):
        @pl.loop(0, 8)
        def _(j):
            b = zat(k) * 8 + j
            moments = MM[slots[c, b]]
            U[pl.ds(pl.multiple_of(b * ROWS, ROWS), ROWS), columns] = scaled_update(
                moments[0].astype(F32), moments[1].astype(F32), PB[b].astype(F32)
            )

        u_across(i, k, columns).start()

    def delta(i, k):
        u_across(i, k, others).wait_recv()
        delta_out[c, rows_of(k), :] = mm(U[rows_of(k), :], QT[...], 1, 0, None).astype(BF16)
        d_twin(i, k, c).start()

    order = (0, -1, 1, -2, 2, -3, 3, 4)
    update(0, 0)
    for s in range(1, 4):
        g_step(s)
        update(2 * s - 1, -s)
        update(2 * s, s)
        for i in range(max(2 * s - 3, 0), 2 * s - 1):
            delta(i, order[i])
    g_step(4)
    update(7, 4)

    holders = ((xl, c), (xl, 1 - c), (1 - xl, c), (1 - xl, 1 - c))
    to_holders = (None, twin, across, diagonal)

    def rows_to(n, matrix, part):
        return remote(GT.at[n], rows_out.at[matrix, :, :, part], es.at[n - 1], er.at[n - 1], to_holders[n])

    for n, (h, k) in enumerate(holders):
        for i in range(CAP):
            GT[n, i] = PB[bucket_of[c, (z * 4 + h * 2 + k) * CAP + i]]
    r_own = pltpu.make_async_copy(GT.at[0], rows_out.at[c, :, :, columns], loc.at[4])
    r_own.start()
    for n in range(1, 4):
        rows_to(n, c, columns).start()
    for i in range(5, 8):
        delta(i, order[i])

    for i, k in enumerate(order):
        d_twin(i, k, c).wait_send()
        u_across(i, k, columns).wait_send()
    for i, k in enumerate(order):
        d_twin(i, -k, 1 - c).wait_recv()
    r_own.wait()
    for n in range(1, 4):
        rows_to(n, c, columns).wait_send()
    rows_to(1, 1 - c, columns).wait_recv()
    rows_to(2, c, others).wait_recv()
    rows_to(3, 1 - c, others).wait_recv()
    t_grads.wait_send()
    half_sum(xl).wait_send()
    for i in range(8):
        x_piece(i).wait_send()
    for i in range(3):
        moments_to(i).wait_send()
    for s in range(4):
        ra(s).wait_send()
        mz(s, 1, -s).wait_send()
        gz(s, 1, -s).wait_send()
    for s in range(3):
        rb(s).wait_send()
        mz(s, -1, s).wait_send()
        gz(s, -1, s).wait_send()


def shards(grads, raw_proj, bucket_owner, first_moment, second_moment):
    matrices, local_rows, features = grads.shape[1:]
    rank = raw_proj.shape[2]
    buckets = bucket_owner.shape[1]
    capacity = first_moment.shape[2]
    slot_total = lax.axis_size("dp") * capacity
    same = bucket_owner[:, :, None] == bucket_owner[:, None, :]
    earlier = jnp.arange(buckets)[None, :] < jnp.arange(buckets)[:, None]
    ranks = jnp.sum(jnp.logical_and(same, earlier).astype(jnp.int32), axis=-1)
    slots = bucket_owner * capacity + ranks
    matches = slots[:, None, :] == jnp.arange(slot_total, dtype=jnp.int32)[None, :, None]
    occupied = jnp.any(matches, axis=2)
    bucket_of = jnp.sum(
        matches.astype(jnp.int32) * jnp.arange(buckets, dtype=jnp.int32)[None, None, :], axis=2
    )
    smem = pl.BlockSpec(memory_space=pltpu.SMEM)
    anywhere = pl.BlockSpec(memory_space=pl.ANY)
    piece = (local_rows // NZ // 2, features)
    dma = pltpu.SemaphoreType.DMA
    weight_delta, grad_rows = pl.pallas_call(
        kernel,
        out_shape=(
            pltpu.VMEM((matrices, local_rows, features), BF16),
            jax.ShapeDtypeStruct((matrices, capacity, ROWS, rank), BF16),
        ),
        in_specs=[smem, smem] + [anywhere] * 4,
        out_specs=(pl.BlockSpec(memory_space=pltpu.VMEM), anywhere),
        scratch_shapes=[
            pltpu.VMEM((features, rank), F32),
            pltpu.VMEM((rank, rank), F32),
            pltpu.VMEM((BLK, 2 * BLK), F32),
            pltpu.VMEM((features, rank), BF16),
            pltpu.VMEM((rank, features), BF16),
            pltpu.VMEM((local_rows, features), BF16),
            pltpu.VMEM((local_rows, features), BF16),
            pltpu.VMEM((4, *piece), BF16),
            pltpu.VMEM((3, *piece), BF16),
            pltpu.VMEM(piece, BF16),
            pltpu.VMEM(piece, BF16),
            pltpu.VMEM((8, *piece), BF16),
            pltpu.VMEM((8, *piece), BF16),
            pltpu.VMEM((local_rows // NZ, features), BF16),
            pltpu.VMEM((slot_total, 2, ROWS, rank // 2), BF16),
            pltpu.VMEM((2, *first_moment.shape), F32),
            pltpu.VMEM((buckets, ROWS, rank // 2), BF16),
            pltpu.VMEM((local_rows, rank), BF16),
            pltpu.VMEM((4, capacity, ROWS, rank // 2), BF16),
            pltpu.VMEM((3, capacity, 2, ROWS, rank // 2), BF16),
            dma((5,)), dma((8,)), dma((8,)), dma((8,)), dma((8,)),
            dma((11,)), dma((11,)), dma((4,)), dma((4,)), dma((7,)), dma((7,)),
            dma((7,)), dma((7,)), dma((9,)), dma((9,)), dma((7,)), dma((7,)), dma((3,)), dma((3,)),
        ],
        compiler_params=pltpu.CompilerParams(
            collective_id=0, has_side_effects=True, vmem_limit_bytes=56 << 20
        ),
        cost_estimate=pl.CostEstimate(
            flops=10_000_000_000, bytes_accessed=16_000_000, transcendentals=1_000_000
        ),
    )(slots, bucket_of, grads, raw_proj, first_moment, second_moment)
    start = lax.axis_index("dp") * capacity
    keep = lax.dynamic_slice_in_dim(occupied, start, capacity, 1)[:, :, None, None]
    first, second = first_moment[:, 0], second_moment[:, 0]
    grad_rows = grad_rows.astype(F32)
    first_out = jnp.where(keep, 0.9 * first + 0.1 * grad_rows, first)[:, None]
    second_out = jnp.where(keep, 0.999 * second + 0.001 * grad_rows * grad_rows, second)[:, None]
    return (weight_delta, first_out, second_out)


def solution(mesh):
    return jax.shard_map(
        shards,
        mesh=mesh,
        in_specs=(
            P("dp", None, "fsdp", None),
            P(None, "fsdp", None),
            P(None, "fsdp"),
            P(None, "fsdp", "dp", None, None),
            P(None, "fsdp", "dp", None, None),
        ),
        out_specs=(
            P(None, "fsdp", None),
            P(None, "fsdp", "dp", None, None),
            P(None, "fsdp", "dp", None, None),
        ),
        check_vma=False,
    )
```

```python
import jax
import jax.numpy as jnp
from jax import lax
from jax.experimental import pallas as pl
from jax.experimental.pallas import tpu as pltpu
from jax.sharding import PartitionSpec as P

HI = lax.Precision.HIGHEST
F32 = jnp.float32
BF16 = jnp.bfloat16
BLK = 128
PAN = 16
NZ, NY, CAP, ROWS = 8, 4, 4, 16


def mm(a, b, ca, cb, precision=HI):
    return lax.dot_general(
        a, b, (((ca,), (cb,)), ((), ())), precision=precision, preferred_element_type=F32
    )


def split(x):
    high = x.astype(BF16).astype(F32)
    middle = (x - high).astype(BF16).astype(F32)
    return high, middle, (x - high) - middle


def mm3(a, b, ca, cb):
    ah, bh = a.astype(BF16), b.astype(BF16)
    al, bl = (a - ah.astype(F32)).astype(BF16), (b - bh.astype(F32)).astype(BF16)
    return mm(ah, bh, ca, cb, None) + (mm(ah, bl, ca, cb, None) + mm(al, bh, ca, cb, None))


def panel(S, g):
    rows = pl.ds(pl.multiple_of(PAN * g, PAN), PAN)
    V, W = S[rows, 0:BLK], S[rows, BLK : 2 * BLK]
    turned = pltpu.roll(V, lax.rem(BLK - PAN * g, BLK), 1)
    C = [jnp.broadcast_to(turned[:, k : k + 1], (PAN, BLK)) for k in range(PAN)]
    sub = lax.broadcasted_iota(jnp.int32, (PAN, BLK), 0)
    lane = lax.broadcasted_iota(jnp.int32, (PAN, BLK), 1)
    pivot = jnp.ones((PAN, BLK), F32)
    for j in range(PAN):
        p = C[j][j : j + 1, :]
        pivot = jnp.where(sub == j, jnp.broadcast_to(p, (PAN, BLK)), pivot)
        if j < PAN - 1:
            m = jnp.where(sub > j, C[j] * jnp.broadcast_to(1.0 / p, (PAN, BLK)), 0.0)
            for k in range(j + 1, PAN):
                C[k] = C[k] - m * jnp.broadcast_to(C[k][j : j + 1, :], (PAN, BLK))
            V = V - m * jnp.broadcast_to(V[j : j + 1, :], (PAN, BLK))
            W = W - m * jnp.broadcast_to(W[j : j + 1, :], (PAN, BLK))
    s = lax.rsqrt(pivot)
    s = s * (1.5 - 0.5 * pivot * s * s)
    VW = jnp.concatenate([V * s, W * s], axis=1)
    S[rows, :] = VW
    high, middle, low = split(VW)
    h, m, l = (jnp.where(lane >= PAN * (g + 1), x[:, 0:BLK], 0.0) for x in (high, middle, low))
    left = jnp.concatenate([h, h, m, h, l, m], axis=0).astype(BF16)
    right = jnp.concatenate([high, middle, high, low, high, middle], axis=0).astype(BF16)
    S[...] = S[...] - mm(left, right, 0, 0, None)


def factor(A, X, S, Q, hooks):
    eye = (
        lax.broadcasted_iota(jnp.int32, (BLK, BLK), 0)
        == lax.broadcasted_iota(jnp.int32, (BLK, BLK), 1)
    ).astype(F32)
    blocks = A.shape[0] // BLK
    for k in range(blocks):
        lo, hi = BLK * k, BLK * k + BLK
        S[:, 0:BLK] = A[lo:hi, lo:hi]
        S[:, BLK : 2 * BLK] = eye

        @pl.loop(0, BLK // PAN)
        def _(g):
            panel(S, g)
            for at, hook in hooks.get(k, {}).items():
                pl.when(g == at)(hook)

        inverse = S[:, BLK : 2 * BLK]
        q = mm3(X[:, lo:hi], inverse, 1, 1)
        Q[:, lo:hi] = q.astype(BF16)
        if k < blocks - 1:
            U = mm(inverse, A[lo:hi, hi:], 1, 0)
            for at in range(hi, A.shape[0], BLK):
                u = U[:, at - hi :]
                A[at : at + BLK, at:] = A[at : at + BLK, at:] - mm(u[:, 0:BLK], u, 0, 0)
            X[:, hi:] = X[:, hi:] - mm3(q, U, 1, 0)


def scaled_update(first, second, g):
    new_first = 0.9 * first + 0.1 * g
    new_second = 0.999 * second + 0.001 * g * g
    scaled = 6.0 * (new_first / (1.0 - 0.9**10)) / (jnp.sqrt(new_second / (1.0 - 0.999**10)) + 1e-08)
    return scaled.astype(BF16)


def kernel(
    slots, bucket_of, grads, raw, first, second, delta_out, rows_out,
    X, A, S, Q, QT, G, T, RA, RB, SA, SB, XS, XR, GS, MM, MO, PB, U, GT, MT,
    loc, ds, dr, us, ur, ys, yr, tws, twr, mzs, mzr, rs, rr, xs, xr, gs, gr, es, er,
):
    dp, f = lax.axis_index("dp"), lax.axis_index("fsdp")
    z, xl, c = dp // 4, lax.rem(dp // 2, 2), lax.rem(dp, 2)
    xh, y = f // NY, lax.rem(f, NY)
    d = 1 - 2 * c

    def zat(k):
        return lax.rem(z + d * k + 2 * NZ, NZ)

    def at_z(k):
        return (zat(k) * 4 + xl * 2 + c, f)

    ahead, behind = at_z(1), at_z(-1)
    across = (z * 4 + (1 - xl) * 2 + c, f)
    twin = (z * 4 + xl * 2 + 1 - c, f)
    diagonal = (z * 4 + (1 - xl) * 2 + 1 - c, f)
    half = Q.shape[1] // 2
    columns = pl.ds(pl.multiple_of(xl * half, half), half)
    others = pl.ds(pl.multiple_of((1 - xl) * half, half), half)
    up, down = (dp, xh * NY + lax.rem(y + 1, NY)), (dp, xh * NY + lax.rem(y + NY - 1, NY))
    mirror = (z * 4 + (1 - xl) * 2 + c, (1 - xh) * NY + y)

    def remote(src, dst, send, recv, to):
        return pltpu.make_async_remote_copy(
            src_ref=src, dst_ref=dst, send_sem=send, recv_sem=recv,
            device_id=to, device_id_type=pl.DeviceIdType.MESH,
        )

    def fblock(h, yy, lo=0, n=128):
        return X.at[pl.ds(pl.multiple_of((h * NY + lax.rem(yy + 2 * NY, NY)) * 128 + lo, 64), n), :]

    def y_send(i):
        what = [
            (fblock(xh, y), up), (fblock(xh, y), down), (fblock(xh, y), mirror),
            (fblock(1 - xh, y, 64, 64), up), (fblock(1 - xh, y, 64, 64), down),
            (fblock(xh, y - 1, 0, 64), up), (fblock(xh, y + 1, 64, 64), down),
            (fblock(1 - xh, y - 1, 0, 64), up), (fblock(1 - xh, y + 1, 64, 64), down),
            (fblock(xh, y - 1, 0, 64), mirror), (fblock(xh, y + 1, 0, 64), mirror),
        ][i]
        return remote(what[0], what[0], ys.at[i], yr.at[i], what[1])

    def y_recv(i):
        what = [
            fblock(xh, y - 1), fblock(xh, y + 1), fblock(1 - xh, y),
            fblock(1 - xh, y - 1, 64, 64), fblock(1 - xh, y + 1, 64, 64),
            fblock(xh, y - 2, 0, 64), fblock(xh, y + 2, 64, 64),
            fblock(1 - xh, y - 2, 0, 64), fblock(1 - xh, y + 2, 64, 64),
            fblock(1 - xh, y - 1, 0, 64), fblock(1 - xh, y + 1, 0, 64),
        ][i]
        remote(what, what, ys.at[i], yr.at[i], up).wait_recv()

    def mblock(k):
        return MM.at[pl.ds(pl.multiple_of(zat(k) * 16, 16), 16)]

    def mz(s, way, k):
        i = s if way > 0 else 4 + s
        return remote(mblock(k), mblock(k), mzs.at[i], mzr.at[i], ahead if way > 0 else behind)

    def m_start():
        mz(0, 1, 0).start()
        mz(0, -1, 0).start()

    def m_step(s):
        mz(s - 1, 1, -s).wait_recv()
        if s < 4:
            mz(s, 1, -s).start()
            mz(s - 1, -1, s).wait_recv()
            if s < 3:
                mz(s, -1, s).start()

    pieces = (4, -3, 3, -2, 2, -1, 1, 0)

    def two_cores(k, h):
        rows = pl.ds(pl.multiple_of(zat(k) * 128 + h * 64, 64), 64)
        return G[rows, :].astype(F32) + T[rows, :].astype(F32)

    def x_piece(i):
        return remote(XS.at[i], XR.at[i], xs.at[i], xr.at[i], across)

    def x_start():
        for i, k in enumerate(pieces):
            XS[i] = two_cores(k, 1 - xl).astype(BF16)
            x_piece(i).start()

    def own(k):
        i = pieces.index(k)
        x_piece(i).wait_recv()
        return two_cores(k, xl) + XR[i].astype(F32)

    def ra(s):
        return remote(SA if s == 0 else RA.at[s - 1], RA.at[s], rs.at[s], rr.at[s], ahead)

    def rb(s):
        return remote(SB if s == 0 else RB.at[s - 1], RB.at[s], rs.at[4 + s], rr.at[4 + s], behind)

    def r_start():
        SA[...] = own(4).astype(BF16)
        ra(0).start()
        SB[...] = own(-3).astype(BF16)
        rb(0).start()

    def r_step(s):
        ra(s - 1).wait_recv()
        RA[s - 1] = (RA[s - 1].astype(F32) + own(4 - s)).astype(BF16)
        ra(s).start()
        if s < 3:
            rb(s - 1).wait_recv()
            RB[s - 1] = (RB[s - 1].astype(F32) + own(s - 3)).astype(BF16)
            rb(s).start()

    def half_sum(h):
        there = GS.at[pl.ds(pl.multiple_of(h * 64, 64), 64), :]
        return remote(there, there, xs.at[8], xr.at[8], across)

    def r_last():
        mine = own(0)
        ra(3).wait_recv()
        rb(2).wait_recv()
        GS[pl.ds(pl.multiple_of(xl * 64, 64), 64), :] = (
            mine + (RA[3].astype(F32) + RB[2].astype(F32))
        ).astype(BF16)
        half_sum(xl).start()

    def r_sum():
        half_sum(1 - xl).wait_recv()

    def pblock(k):
        return PB.at[pl.ds(pl.multiple_of(zat(k) * 8, 8), 8)]

    def gz(s, way, k):
        i = s if way > 0 else 4 + s
        return remote(pblock(k), pblock(k), gs.at[i], gr.at[i], ahead if way > 0 else behind)

    def g_start():
        part = mm(GS[...], Q[:, columns], 1, 0, None)
        pblock(0)[...] = part.reshape(8, ROWS, part.shape[1]).astype(BF16)
        gz(0, 1, 0).start()
        gz(0, -1, 0).start()

    def g_step(s):
        gz(s - 1, 1, -s).wait_recv()
        if s < 4:
            gz(s, 1, -s).start()
            gz(s - 1, -1, s).wait_recv()
            if s < 3:
                gz(s, -1, s).start()

    partners = (ahead, behind, across, twin, diagonal, up, down, mirror)
    barrier = pltpu.get_barrier_semaphore()
    for to in partners:
        pl.semaphore_signal(barrier, inc=1, device_id=to, device_id_type=pl.DeviceIdType.MESH)
    own_raw = pltpu.make_async_copy(raw.at[c], fblock(xh, y), loc.at[0])
    own_grads = pltpu.make_async_copy(grads.at[0, c], G, loc.at[1])
    own_raw.start()
    own_grads.start()
    own_moments = [
        pltpu.make_async_copy(ref, MO.at[i], loc.at[2 + i]) for i, ref in enumerate((first, second))
    ]
    for copy in own_moments:
        copy.start()
    def place(h, k):
        return MM.at[pl.ds(pl.multiple_of((z * 4 + h * 2 + k) * CAP, CAP), CAP)]

    targets = ((twin, xl, 1 - c), (across, 1 - xl, c), (diagonal, 1 - xl, 1 - c))

    def moments_to(i):
        to, h, k = targets[i]
        return remote(MT.at[i], place(xl, c), tws.at[1 + i], twr.at[1 + i], to)

    for i, copy in enumerate(own_moments):
        copy.wait()
        place(xl, c)[:, i] = MO[i, c, 0, :, :, columns].astype(BF16)
        MT[0, :, i] = MO[i, 1 - c, 0, :, :, columns].astype(BF16)
        MT[1, :, i] = MO[i, c, 0, :, :, others].astype(BF16)
        MT[2, :, i] = MO[i, 1 - c, 0, :, :, others].astype(BF16)
    own_raw.wait()
    pl.semaphore_wait(barrier, len(partners))

    for i in range(3):
        y_send(i).start()
    t_grads = remote(grads.at[0, 1 - c], T, tws.at[0], twr.at[0], twin)
    for i in range(3):
        moments_to(i).start()
    t_grads.start()
    for i, (to, h, k) in enumerate(targets):
        remote(MT.at[i], place(h, k), tws.at[1 + i], twr.at[1 + i], to).wait_recv()
    m_start()
    own_grads.wait()
    t_grads.wait_recv()
    x_start()

    def gram(yy, add):
        part = jnp.concatenate([fblock(xh, yy)[...], fblock(1 - xh, yy)[...]], axis=0)
        for lo in range(0, part.shape[1], BLK):
            product = mm(part[:, lo : lo + BLK], part[:, lo:], 0, 0)
            A[lo : lo + BLK, lo:] = A[lo : lo + BLK, lo:] + product if add else product

    for arrived, sends in ((2, (3, 4)), (0, (5, 9)), (1, (6, 10))):
        y_recv(arrived)
        for i in sends:
            y_send(i).start()
    gram(y, False)
    y_recv(4)
    y_send(8).start()
    y_recv(9)
    y_send(7).start()
    m_step(1)
    r_start()
    y_recv(3)
    gram(y - 1, True)
    y_recv(10)
    gram(y + 1, True)
    for i in range(5, 9):
        y_recv(i)
    gram(y + 2, True)
    for i in range(11):
        y_send(i).wait_send()

    hooks = {
        0: {2: lambda: r_step(1), 6: lambda: m_step(2)},
        1: {2: lambda: r_step(2)},
        2: {0: lambda: r_step(3), 3: lambda: m_step(3), 7: r_last},
        3: {7: r_sum},
    }
    factor(A, X, S, Q, hooks)
    g_start()
    m_step(4)

    for lo in range(0, Q.shape[1], BLK):
        QT[lo : lo + BLK, :] = Q[:, lo : lo + BLK].T

    def rows_of(k):
        return pl.ds(pl.multiple_of(zat(k) * 128, 128), 128)

    def u_across(i, k, part):
        there = U.at[rows_of(k), part]
        return remote(there, there, us.at[i], ur.at[i], across)

    def d_twin(i, k, at):
        there = delta_out.at[at, rows_of(k), :]
        return remote(there, there, ds.at[i], dr.at[i], twin)

    def update(i, k):
        @pl.loop(0, 8)
        def _(j):
            b = zat(k) * 8 + j
            moments = MM[slots[c, b]]
            U[pl.ds(pl.multiple_of(b * ROWS, ROWS), ROWS), columns] = scaled_update(
                moments[0].astype(F32), moments[1].astype(F32), PB[b].astype(F32)
            )

        u_across(i, k, columns).start()

    def delta(i, k):
        u_across(i, k, others).wait_recv()
        delta_out[c, rows_of(k), :] = mm(U[rows_of(k), :], QT[...], 1, 0, None).astype(BF16)
        d_twin(i, k, c).start()

    order = (0, -1, 1, -2, 2, -3, 3, 4)
    update(0, 0)
    for s in range(1, 4):
        g_step(s)
        update(2 * s - 1, -s)
        update(2 * s, s)
        for i in range(max(2 * s - 3, 0), 2 * s - 1):
            delta(i, order[i])
    g_step(4)
    update(7, 4)

    holders = ((xl, c), (xl, 1 - c), (1 - xl, c), (1 - xl, 1 - c))
    to_holders = (None, twin, across, diagonal)

    def rows_to(n, matrix, part):
        return remote(GT.at[n], rows_out.at[matrix, :, :, part], es.at[n - 1], er.at[n - 1], to_holders[n])

    for n, (h, k) in enumerate(holders):
        for i in range(CAP):
            GT[n, i] = PB[bucket_of[c, (z * 4 + h * 2 + k) * CAP + i]]
    r_own = pltpu.make_async_copy(GT.at[0], rows_out.at[c, :, :, columns], loc.at[4])
    r_own.start()
    for n in range(1, 4):
        rows_to(n, c, columns).start()
    for i in range(5, 8):
        delta(i, order[i])

    for i, k in enumerate(order):
        d_twin(i, k, c).wait_send()
        u_across(i, k, columns).wait_send()
    for i, k in enumerate(order):
        d_twin(i, -k, 1 - c).wait_recv()
    r_own.wait()
    for n in range(1, 4):
        rows_to(n, c, columns).wait_send()
    rows_to(1, 1 - c, columns).wait_recv()
    rows_to(2, c, others).wait_recv()
    rows_to(3, 1 - c, others).wait_recv()
    t_grads.wait_send()
    half_sum(xl).wait_send()
    for i in range(8):
        x_piece(i).wait_send()
    for i in range(3):
        moments_to(i).wait_send()
    for s in range(4):
        ra(s).wait_send()
        mz(s, 1, -s).wait_send()
        gz(s, 1, -s).wait_send()
    for s in range(3):
        rb(s).wait_send()
        mz(s, -1, s).wait_send()
        gz(s, -1, s).wait_send()


def shards(grads, raw_proj, bucket_owner, first_moment, second_moment):
    matrices, local_rows, features = grads.shape[1:]
    rank = raw_proj.shape[2]
    buckets = bucket_owner.shape[1]
    capacity = first_moment.shape[2]
    slot_total = lax.axis_size("dp") * capacity
    same = bucket_owner[:, :, None] == bucket_owner[:, None, :]
    earlier = jnp.arange(buckets)[None, :] < jnp.arange(buckets)[:, None]
    ranks = jnp.sum(jnp.logical_and(same, earlier).astype(jnp.int32), axis=-1)
    slots = bucket_owner * capacity + ranks
    matches = slots[:, None, :] == jnp.arange(slot_total, dtype=jnp.int32)[None, :, None]
    occupied = jnp.any(matches, axis=2)
    bucket_of = jnp.sum(
        matches.astype(jnp.int32) * jnp.arange(buckets, dtype=jnp.int32)[None, None, :], axis=2
    )
    smem = pl.BlockSpec(memory_space=pltpu.SMEM)
    anywhere = pl.BlockSpec(memory_space=pl.ANY)
    piece = (local_rows // NZ // 2, features)
    dma = pltpu.SemaphoreType.DMA
    weight_delta, grad_rows = pl.pallas_call(
        kernel,
        out_shape=(
            pltpu.VMEM((matrices, local_rows, features), BF16),
            jax.ShapeDtypeStruct((matrices, capacity, ROWS, rank), BF16),
        ),
        in_specs=[smem, smem] + [anywhere] * 4,
        out_specs=(pl.BlockSpec(memory_space=pltpu.VMEM), anywhere),
        scratch_shapes=[
            pltpu.VMEM((features, rank), F32),
            pltpu.VMEM((rank, rank), F32),
            pltpu.VMEM((BLK, 2 * BLK), F32),
            pltpu.VMEM((features, rank), BF16),
            pltpu.VMEM((rank, features), BF16),
            pltpu.VMEM((local_rows, features), BF16),
            pltpu.VMEM((local_rows, features), BF16),
            pltpu.VMEM((4, *piece), BF16),
            pltpu.VMEM((3, *piece), BF16),
            pltpu.VMEM(piece, BF16),
            pltpu.VMEM(piece, BF16),
            pltpu.VMEM((8, *piece), BF16),
            pltpu.VMEM((8, *piece), BF16),
            pltpu.VMEM((local_rows // NZ, features), BF16),
            pltpu.VMEM((slot_total, 2, ROWS, rank // 2), BF16),
            pltpu.VMEM((2, *first_moment.shape), F32),
            pltpu.VMEM((buckets, ROWS, rank // 2), BF16),
            pltpu.VMEM((local_rows, rank), BF16),
            pltpu.VMEM((4, capacity, ROWS, rank // 2), BF16),
            pltpu.VMEM((3, capacity, 2, ROWS, rank // 2), BF16),
            dma((5,)), dma((8,)), dma((8,)), dma((8,)), dma((8,)),
            dma((11,)), dma((11,)), dma((4,)), dma((4,)), dma((7,)), dma((7,)),
            dma((7,)), dma((7,)), dma((9,)), dma((9,)), dma((7,)), dma((7,)), dma((3,)), dma((3,)),
        ],
        compiler_params=pltpu.CompilerParams(
            collective_id=0, has_side_effects=True, vmem_limit_bytes=56 << 20
        ),
        cost_estimate=pl.CostEstimate(
            flops=10_000_000_000, bytes_accessed=16_000_000, transcendentals=1_000_000
        ),
    )(slots, bucket_of, grads, raw_proj, first_moment, second_moment)
    start = lax.axis_index("dp") * capacity
    keep = lax.dynamic_slice_in_dim(occupied, start, capacity, 1)[:, :, None, None]
    first, second = first_moment[:, 0], second_moment[:, 0]
    grad_rows = grad_rows.astype(F32)
    first_out = jnp.where(keep, 0.9 * first + 0.1 * grad_rows, first)[:, None]
    second_out = jnp.where(keep, 0.999 * second + 0.001 * grad_rows * grad_rows, second)[:, None]
    return (weight_delta, first_out, second_out)


def solution(mesh):
    return jax.shard_map(
        shards,
        mesh=mesh,
        in_specs=(
            P("dp", None, "fsdp", None),
            P(None, "fsdp", None),
            P(None, "fsdp"),
            P(None, "fsdp", "dp", None, None),
            P(None, "fsdp", "dp", None, None),
        ),
        out_specs=(
            P(None, "fsdp", None),
            P(None, "fsdp", "dp", None, None),
            P(None, "fsdp", "dp", None, None),
        ),
        check_vma=False,
    )
```

```python
import jax
import jax.numpy as jnp
from jax import lax
from jax.experimental import pallas as pl
from jax.experimental.pallas import tpu as pltpu
from jax.sharding import PartitionSpec as P

HI = lax.Precision.HIGHEST
F32 = jnp.float32
BF16 = jnp.bfloat16
BLK = 128
PAN = 16
NZ, NY, CAP, ROWS = 8, 4, 4, 16


def mm(a, b, ca, cb, precision=HI):
    return lax.dot_general(
        a, b, (((ca,), (cb,)), ((), ())), precision=precision, preferred_element_type=F32
    )


def split(x):
    high = x.astype(BF16).astype(F32)
    middle = (x - high).astype(BF16).astype(F32)
    return high, middle, (x - high) - middle


def mm3(a, b, ca, cb):
    ah, bh = a.astype(BF16), b.astype(BF16)
    al, bl = (a - ah.astype(F32)).astype(BF16), (b - bh.astype(F32)).astype(BF16)
    return mm(ah, bh, ca, cb, None) + (mm(ah, bl, ca, cb, None) + mm(al, bh, ca, cb, None))


def panel(S, g):
    rows = pl.ds(pl.multiple_of(PAN * g, PAN), PAN)
    V, W = S[rows, 0:BLK], S[rows, BLK : 2 * BLK]
    turned = pltpu.roll(V, lax.rem(BLK - PAN * g, BLK), 1)
    C = [jnp.broadcast_to(turned[:, k : k + 1], (PAN, BLK)) for k in range(PAN)]
    sub = lax.broadcasted_iota(jnp.int32, (PAN, BLK), 0)
    lane = lax.broadcasted_iota(jnp.int32, (PAN, BLK), 1)
    pivot = jnp.ones((PAN, BLK), F32)
    for j in range(PAN):
        p = C[j][j : j + 1, :]
        pivot = jnp.where(sub == j, jnp.broadcast_to(p, (PAN, BLK)), pivot)
        if j < PAN - 1:
            m = jnp.where(sub > j, C[j] * jnp.broadcast_to(1.0 / p, (PAN, BLK)), 0.0)
            for k in range(j + 1, PAN):
                C[k] = C[k] - m * jnp.broadcast_to(C[k][j : j + 1, :], (PAN, BLK))
            V = V - m * jnp.broadcast_to(V[j : j + 1, :], (PAN, BLK))
            W = W - m * jnp.broadcast_to(W[j : j + 1, :], (PAN, BLK))
    s = lax.rsqrt(pivot)
    s = s * (1.5 - 0.5 * pivot * s * s)
    VW = jnp.concatenate([V * s, W * s], axis=1)
    S[rows, :] = VW
    high, middle, low = split(VW)
    h, m, l = (jnp.where(lane >= PAN * (g + 1), x[:, 0:BLK], 0.0) for x in (high, middle, low))
    left = jnp.concatenate([h, h, m, h, l, m], axis=0).astype(BF16)
    right = jnp.concatenate([high, middle, high, low, high, middle], axis=0).astype(BF16)
    S[...] = S[...] - mm(left, right, 0, 0, None)


def factor(A, X, S, Q, hooks):
    eye = (
        lax.broadcasted_iota(jnp.int32, (BLK, BLK), 0)
        == lax.broadcasted_iota(jnp.int32, (BLK, BLK), 1)
    ).astype(F32)
    blocks = A.shape[0] // BLK
    for k in range(blocks):
        lo, hi = BLK * k, BLK * k + BLK
        S[:, 0:BLK] = A[lo:hi, lo:hi]
        S[:, BLK : 2 * BLK] = eye

        @pl.loop(0, BLK // PAN)
        def _(g):
            panel(S, g)
            for at, hook in hooks.get(k, {}).items():
                pl.when(g == at)(hook)

        inverse = S[:, BLK : 2 * BLK]
        q = mm3(X[:, lo:hi], inverse, 1, 1)
        Q[:, lo:hi] = q.astype(BF16)
        if k < blocks - 1:
            U = mm(inverse, A[lo:hi, hi:], 1, 0)
            for at in range(hi, A.shape[0], BLK):
                u = U[:, at - hi :]
                A[at : at + BLK, at:] = A[at : at + BLK, at:] - mm(u[:, 0:BLK], u, 0, 0)
            X[:, hi:] = X[:, hi:] - mm3(q, U, 1, 0)


def scaled_update(first, second, g):
    new_first = 0.9 * first + 0.1 * g
    new_second = 0.999 * second + 0.001 * g * g
    scaled = 6.0 * (new_first / (1.0 - 0.9**10)) / (jnp.sqrt(new_second / (1.0 - 0.999**10)) + 1e-08)
    return scaled.astype(BF16)


def kernel(
    slots, bucket_of, grads, raw, first, second, delta_out, rows_out,
    X, A, S, Q, QT, G, T, RA, RB, SA, SB, XS, XR, GS, MM, MO, PB, U, GT, MT,
    loc, ds, dr, us, ur, ys, yr, tws, twr, mzs, mzr, rs, rr, xs, xr, gs, gr, es, er,
):
    dp, f = lax.axis_index("dp"), lax.axis_index("fsdp")
    z, xl, c = dp // 4, lax.rem(dp // 2, 2), lax.rem(dp, 2)
    xh, y = f // NY, lax.rem(f, NY)
    d = 1 - 2 * c

    def zat(k):
        return lax.rem(z + d * k + 2 * NZ, NZ)

    def at_z(k):
        return (zat(k) * 4 + xl * 2 + c, f)

    ahead, behind = at_z(1), at_z(-1)
    across = (z * 4 + (1 - xl) * 2 + c, f)
    twin = (z * 4 + xl * 2 + 1 - c, f)
    diagonal = (z * 4 + (1 - xl) * 2 + 1 - c, f)
    half = Q.shape[1] // 2
    columns = pl.ds(pl.multiple_of(xl * half, half), half)
    others = pl.ds(pl.multiple_of((1 - xl) * half, half), half)
    up, down = (dp, xh * NY + lax.rem(y + 1, NY)), (dp, xh * NY + lax.rem(y + NY - 1, NY))
    mirror = (z * 4 + (1 - xl) * 2 + c, (1 - xh) * NY + y)

    def remote(src, dst, send, recv, to):
        return pltpu.make_async_remote_copy(
            src_ref=src, dst_ref=dst, send_sem=send, recv_sem=recv,
            device_id=to, device_id_type=pl.DeviceIdType.MESH,
        )

    def fblock(h, yy, lo=0, n=128):
        return X.at[pl.ds(pl.multiple_of((h * NY + lax.rem(yy + 2 * NY, NY)) * 128 + lo, 64), n), :]

    def y_send(i):
        what = [
            (fblock(xh, y), up), (fblock(xh, y), down), (fblock(xh, y), mirror),
            (fblock(1 - xh, y, 64, 64), up), (fblock(1 - xh, y, 64, 64), down),
            (fblock(xh, y - 1, 0, 64), up), (fblock(xh, y + 1, 64, 64), down),
            (fblock(1 - xh, y - 1, 0, 64), up), (fblock(1 - xh, y + 1, 64, 64), down),
            (fblock(xh, y - 1, 0, 64), mirror), (fblock(xh, y + 1, 0, 64), mirror),
        ][i]
        return remote(what[0], what[0], ys.at[i], yr.at[i], what[1])

    def y_recv(i):
        what = [
            fblock(xh, y - 1), fblock(xh, y + 1), fblock(1 - xh, y),
            fblock(1 - xh, y - 1, 64, 64), fblock(1 - xh, y + 1, 64, 64),
            fblock(xh, y - 2, 0, 64), fblock(xh, y + 2, 64, 64),
            fblock(1 - xh, y - 2, 0, 64), fblock(1 - xh, y + 2, 64, 64),
            fblock(1 - xh, y - 1, 0, 64), fblock(1 - xh, y + 1, 0, 64),
        ][i]
        remote(what, what, ys.at[i], yr.at[i], up).wait_recv()

    def mblock(k):
        return MM.at[pl.ds(pl.multiple_of(zat(k) * 16, 16), 16)]

    def mz(s, way, k):
        i = s if way > 0 else 4 + s
        return remote(mblock(k), mblock(k), mzs.at[i], mzr.at[i], ahead if way > 0 else behind)

    def m_start():
        mz(0, 1, 0).start()
        mz(0, -1, 0).start()

    def m_step(s):
        mz(s - 1, 1, -s).wait_recv()
        if s < 4:
            mz(s, 1, -s).start()
            mz(s - 1, -1, s).wait_recv()
            if s < 3:
                mz(s, -1, s).start()

    pieces = (4, -3, 3, -2, 2, -1, 1, 0)

    def two_cores(k, h):
        rows = pl.ds(pl.multiple_of(zat(k) * 128 + h * 64, 64), 64)
        return G[rows, :].astype(F32) + T[rows, :].astype(F32)

    def x_piece(i):
        return remote(XS.at[i], XR.at[i], xs.at[i], xr.at[i], across)

    def x_start():
        for i, k in enumerate(pieces):
            XS[i] = two_cores(k, 1 - xl).astype(BF16)
            x_piece(i).start()

    def own(k):
        i = pieces.index(k)
        x_piece(i).wait_recv()
        return two_cores(k, xl) + XR[i].astype(F32)

    def ra(s):
        return remote(SA if s == 0 else RA.at[s - 1], RA.at[s], rs.at[s], rr.at[s], ahead)

    def rb(s):
        return remote(SB if s == 0 else RB.at[s - 1], RB.at[s], rs.at[4 + s], rr.at[4 + s], behind)

    def r_start():
        SA[...] = own(4).astype(BF16)
        ra(0).start()
        SB[...] = own(-3).astype(BF16)
        rb(0).start()

    def r_step(s):
        ra(s - 1).wait_recv()
        RA[s - 1] = (RA[s - 1].astype(F32) + own(4 - s)).astype(BF16)
        ra(s).start()
        if s < 3:
            rb(s - 1).wait_recv()
            RB[s - 1] = (RB[s - 1].astype(F32) + own(s - 3)).astype(BF16)
            rb(s).start()

    def half_sum(h):
        there = GS.at[pl.ds(pl.multiple_of(h * 64, 64), 64), :]
        return remote(there, there, xs.at[8], xr.at[8], across)

    def r_last():
        mine = own(0)
        ra(3).wait_recv()
        rb(2).wait_recv()
        GS[pl.ds(pl.multiple_of(xl * 64, 64), 64), :] = (
            mine + (RA[3].astype(F32) + RB[2].astype(F32))
        ).astype(BF16)
        half_sum(xl).start()

    def r_sum():
        half_sum(1 - xl).wait_recv()

    def pblock(k):
        return PB.at[pl.ds(pl.multiple_of(zat(k) * 8, 8), 8)]

    def gz(s, way, k):
        i = s if way > 0 else 4 + s
        return remote(pblock(k), pblock(k), gs.at[i], gr.at[i], ahead if way > 0 else behind)

    def g_start():
        part = mm(GS[...], Q[:, columns], 1, 0, None)
        pblock(0)[...] = part.reshape(8, ROWS, part.shape[1]).astype(BF16)
        gz(0, 1, 0).start()
        gz(0, -1, 0).start()

    def g_step(s):
        gz(s - 1, 1, -s).wait_recv()
        if s < 4:
            gz(s, 1, -s).start()
            gz(s - 1, -1, s).wait_recv()
            if s < 3:
                gz(s, -1, s).start()

    partners = (ahead, behind, across, twin, diagonal, up, down, mirror)
    barrier = pltpu.get_barrier_semaphore()
    for to in partners:
        pl.semaphore_signal(barrier, inc=1, device_id=to, device_id_type=pl.DeviceIdType.MESH)
    own_raw = pltpu.make_async_copy(raw.at[c], fblock(xh, y), loc.at[0])
    own_grads = pltpu.make_async_copy(grads.at[0, c], G, loc.at[1])
    own_raw.start()
    own_grads.start()
    own_moments = [
        pltpu.make_async_copy(ref, MO.at[i], loc.at[2 + i]) for i, ref in enumerate((first, second))
    ]
    for copy in own_moments:
        copy.start()
    def place(h, k):
        return MM.at[pl.ds(pl.multiple_of((z * 4 + h * 2 + k) * CAP, CAP), CAP)]

    targets = ((twin, xl, 1 - c), (across, 1 - xl, c), (diagonal, 1 - xl, 1 - c))

    def moments_to(i):
        to, h, k = targets[i]
        return remote(MT.at[i], place(xl, c), tws.at[1 + i], twr.at[1 + i], to)

    for i, copy in enumerate(own_moments):
        copy.wait()
        place(xl, c)[:, i] = MO[i, c, 0, :, :, columns].astype(BF16)
        MT[0, :, i] = MO[i, 1 - c, 0, :, :, columns].astype(BF16)
        MT[1, :, i] = MO[i, c, 0, :, :, others].astype(BF16)
        MT[2, :, i] = MO[i, 1 - c, 0, :, :, others].astype(BF16)
    own_raw.wait()
    pl.semaphore_wait(barrier, len(partners))

    for i in range(3):
        y_send(i).start()
    t_grads = remote(grads.at[0, 1 - c], T, tws.at[0], twr.at[0], twin)
    for i in range(3):
        moments_to(i).start()
    t_grads.start()
    for i, (to, h, k) in enumerate(targets):
        remote(MT.at[i], place(h, k), tws.at[1 + i], twr.at[1 + i], to).wait_recv()
    m_start()
    own_grads.wait()
    t_grads.wait_recv()
    x_start()

    def gram(yy, add):
        part = jnp.concatenate([fblock(xh, yy)[...], fblock(1 - xh, yy)[...]], axis=0)
        for lo in range(0, part.shape[1], BLK):
            product = mm(part[:, lo : lo + BLK], part[:, lo:], 0, 0)
            A[lo : lo + BLK, lo:] = A[lo : lo + BLK, lo:] + product if add else product

    for arrived, sends in ((2, (3, 4)), (0, (5, 9)), (1, (6, 10))):
        y_recv(arrived)
        for i in sends:
            y_send(i).start()
    gram(y, False)
    y_recv(4)
    y_send(8).start()
    y_recv(9)
    y_send(7).start()
    m_step(1)
    r_start()
    y_recv(3)
    gram(y - 1, True)
    y_recv(10)
    gram(y + 1, True)
    for i in range(5, 9):
        y_recv(i)
    gram(y + 2, True)
    for i in range(11):
        y_send(i).wait_send()

    hooks = {
        0: {3: lambda: r_step(1), 7: lambda: m_step(2)},
        1: {4: lambda: r_step(2)},
        2: {2: lambda: r_step(3), 5: lambda: m_step(3)},
        3: {1: r_last},
    }
    factor(A, X, S, Q, hooks)
    r_sum()
    g_start()
    m_step(4)

    for lo in range(0, Q.shape[1], BLK):
        QT[lo : lo + BLK, :] = Q[:, lo : lo + BLK].T

    def rows_of(k):
        return pl.ds(pl.multiple_of(zat(k) * 128, 128), 128)

    def u_across(i, k, part):
        there = U.at[rows_of(k), part]
        return remote(there, there, us.at[i], ur.at[i], across)

    def d_twin(i, k, at):
        there = delta_out.at[at, rows_of(k), :]
        return remote(there, there, ds.at[i], dr.at[i], twin)

    def update(i, k):
        @pl.loop(0, 8)
        def _(j):
            b = zat(k) * 8 + j
            moments = MM[slots[c, b]]
            U[pl.ds(pl.multiple_of(b * ROWS, ROWS), ROWS), columns] = scaled_update(
                moments[0].astype(F32), moments[1].astype(F32), PB[b].astype(F32)
            )

        u_across(i, k, columns).start()

    def delta(i, k):
        u_across(i, k, others).wait_recv()
        delta_out[c, rows_of(k), :] = mm(U[rows_of(k), :], QT[...], 1, 0, None).astype(BF16)
        d_twin(i, k, c).start()

    order = (0, -1, 1, -2, 2, -3, 3, 4)
    update(0, 0)
    for s in range(1, 4):
        g_step(s)
        update(2 * s - 1, -s)
        update(2 * s, s)
        for i in range(max(2 * s - 3, 0), 2 * s - 1):
            delta(i, order[i])
    g_step(4)
    update(7, 4)

    holders = ((xl, c), (xl, 1 - c), (1 - xl, c), (1 - xl, 1 - c))
    to_holders = (None, twin, across, diagonal)

    def rows_to(n, matrix, part):
        return remote(GT.at[n], rows_out.at[matrix, :, :, part], es.at[n - 1], er.at[n - 1], to_holders[n])

    for n, (h, k) in enumerate(holders):
        for i in range(CAP):
            GT[n, i] = PB[bucket_of[c, (z * 4 + h * 2 + k) * CAP + i]]
    r_own = pltpu.make_async_copy(GT.at[0], rows_out.at[c, :, :, columns], loc.at[4])
    r_own.start()
    for n in range(1, 4):
        rows_to(n, c, columns).start()
    for i in range(5, 8):
        delta(i, order[i])

    for i, k in enumerate(order):
        d_twin(i, k, c).wait_send()
        u_across(i, k, columns).wait_send()
    for i, k in enumerate(order):
        d_twin(i, -k, 1 - c).wait_recv()
    r_own.wait()
    for n in range(1, 4):
        rows_to(n, c, columns).wait_send()
    rows_to(1, 1 - c, columns).wait_recv()
    rows_to(2, c, others).wait_recv()
    rows_to(3, 1 - c, others).wait_recv()
    t_grads.wait_send()
    half_sum(xl).wait_send()
    for i in range(8):
        x_piece(i).wait_send()
    for i in range(3):
        moments_to(i).wait_send()
    for s in range(4):
        ra(s).wait_send()
        mz(s, 1, -s).wait_send()
        gz(s, 1, -s).wait_send()
    for s in range(3):
        rb(s).wait_send()
        mz(s, -1, s).wait_send()
        gz(s, -1, s).wait_send()


def shards(grads, raw_proj, bucket_owner, first_moment, second_moment):
    matrices, local_rows, features = grads.shape[1:]
    rank = raw_proj.shape[2]
    buckets = bucket_owner.shape[1]
    capacity = first_moment.shape[2]
    slot_total = lax.axis_size("dp") * capacity
    same = bucket_owner[:, :, None] == bucket_owner[:, None, :]
    index = jnp.arange(buckets)
    earlier = index[None, :] < index[:, None]
    terms = jnp.logical_and(same, earlier).astype(jnp.int32) + jnp.where(
        index[None, :] == index[:, None], capacity * bucket_owner[:, None, :], 0
    )
    slots = jnp.sum(terms, axis=-1)
    matches = slots[:, None, :] == jnp.arange(slot_total, dtype=jnp.int32)[None, :, None]
    occupied = jnp.any(matches, axis=2)
    bucket_of = jnp.sum(
        matches.astype(jnp.int32) * jnp.arange(buckets, dtype=jnp.int32)[None, None, :], axis=2
    )
    smem = pl.BlockSpec(memory_space=pltpu.SMEM)
    anywhere = pl.BlockSpec(memory_space=pl.ANY)
    piece = (local_rows // NZ // 2, features)
    dma = pltpu.SemaphoreType.DMA
    weight_delta, grad_rows = pl.pallas_call(
        kernel,
        out_shape=(
            pltpu.VMEM((matrices, local_rows, features), BF16),
            jax.ShapeDtypeStruct((matrices, capacity, ROWS, rank), BF16),
        ),
        in_specs=[smem, smem] + [anywhere] * 4,
        out_specs=(pl.BlockSpec(memory_space=pltpu.VMEM), anywhere),
        scratch_shapes=[
            pltpu.VMEM((features, rank), F32),
            pltpu.VMEM((rank, rank), F32),
            pltpu.VMEM((BLK, 2 * BLK), F32),
            pltpu.VMEM((features, rank), BF16),
            pltpu.VMEM((rank, features), BF16),
            pltpu.VMEM((local_rows, features), BF16),
            pltpu.VMEM((local_rows, features), BF16),
            pltpu.VMEM((4, *piece), BF16),
            pltpu.VMEM((3, *piece), BF16),
            pltpu.VMEM(piece, BF16),
            pltpu.VMEM(piece, BF16),
            pltpu.VMEM((8, *piece), BF16),
            pltpu.VMEM((8, *piece), BF16),
            pltpu.VMEM((local_rows // NZ, features), BF16),
            pltpu.VMEM((slot_total, 2, ROWS, rank // 2), BF16),
            pltpu.VMEM((2, *first_moment.shape), F32),
            pltpu.VMEM((buckets, ROWS, rank // 2), BF16),
            pltpu.VMEM((local_rows, rank), BF16),
            pltpu.VMEM((4, capacity, ROWS, rank // 2), BF16),
            pltpu.VMEM((3, capacity, 2, ROWS, rank // 2), BF16),
            dma((5,)), dma((8,)), dma((8,)), dma((8,)), dma((8,)),
            dma((11,)), dma((11,)), dma((4,)), dma((4,)), dma((7,)), dma((7,)),
            dma((7,)), dma((7,)), dma((9,)), dma((9,)), dma((7,)), dma((7,)), dma((3,)), dma((3,)),
        ],
        compiler_params=pltpu.CompilerParams(
            collective_id=0, has_side_effects=True, vmem_limit_bytes=56 << 20
        ),
        cost_estimate=pl.CostEstimate(
            flops=10_000_000_000, bytes_accessed=16_000_000, transcendentals=1_000_000
        ),
    )(slots, bucket_of, grads, raw_proj, first_moment, second_moment)
    start = lax.axis_index("dp") * capacity
    keep = lax.dynamic_slice_in_dim(occupied, start, capacity, 1)[:, :, None, None]
    first, second = first_moment[:, 0], second_moment[:, 0]
    grad_rows = grad_rows.astype(F32)
    first_out = jnp.where(keep, 0.9 * first + 0.1 * grad_rows, first)[:, None]
    second_out = jnp.where(keep, 0.999 * second + 0.001 * grad_rows * grad_rows, second)[:, None]
    return (weight_delta, first_out, second_out)


def solution(mesh):
    return jax.shard_map(
        shards,
        mesh=mesh,
        in_specs=(
            P("dp", None, "fsdp", None),
            P(None, "fsdp", None),
            P(None, "fsdp"),
            P(None, "fsdp", "dp", None, None),
            P(None, "fsdp", "dp", None, None),
        ),
        out_specs=(
            P(None, "fsdp", None),
            P(None, "fsdp", "dp", None, None),
            P(None, "fsdp", "dp", None, None),
        ),
        check_vma=False,
    )
```

```python
import jax
import jax.numpy as jnp
from jax import lax
from jax.experimental import pallas as pl
from jax.experimental.pallas import tpu as pltpu
from jax.sharding import PartitionSpec as P

HI = lax.Precision.HIGHEST
F32 = jnp.float32
BF16 = jnp.bfloat16
BLK = 128
PAN = 16
NZ, NY, CAP, ROWS = 8, 4, 4, 16


def mm(a, b, ca, cb, precision=HI):
    return lax.dot_general(
        a, b, (((ca,), (cb,)), ((), ())), precision=precision, preferred_element_type=F32
    )


def split(x):
    high = x.astype(BF16).astype(F32)
    middle = (x - high).astype(BF16).astype(F32)
    return high, middle, (x - high) - middle


def mm3(a, b, ca, cb):
    ah, bh = a.astype(BF16), b.astype(BF16)
    al, bl = (a - ah.astype(F32)).astype(BF16), (b - bh.astype(F32)).astype(BF16)
    left = jnp.concatenate([ah, ah, al], axis=ca)
    return mm(left, jnp.concatenate([bh, bl, bh], axis=cb), ca, cb, None)


def panel(S, g):
    rows = pl.ds(pl.multiple_of(PAN * g, PAN), PAN)
    V, W = S[rows, 0:BLK], S[rows, BLK : 2 * BLK]
    turned = pltpu.roll(V, lax.rem(BLK - PAN * g, BLK), 1)
    C = [jnp.broadcast_to(turned[:, k : k + 1], (PAN, BLK)) for k in range(PAN)]
    sub = lax.broadcasted_iota(jnp.int32, (PAN, BLK), 0)
    lane = lax.broadcasted_iota(jnp.int32, (PAN, BLK), 1)
    pivot = jnp.ones((PAN, BLK), F32)
    for j in range(PAN):
        p = C[j][j : j + 1, :]
        pivot = jnp.where(sub == j, jnp.broadcast_to(p, (PAN, BLK)), pivot)
        if j < PAN - 1:
            m = jnp.where(sub > j, C[j] * jnp.broadcast_to(1.0 / p, (PAN, BLK)), 0.0)
            for k in range(j + 1, PAN):
                C[k] = C[k] - m * jnp.broadcast_to(C[k][j : j + 1, :], (PAN, BLK))
            V = V - m * jnp.broadcast_to(V[j : j + 1, :], (PAN, BLK))
            W = W - m * jnp.broadcast_to(W[j : j + 1, :], (PAN, BLK))
    s = lax.rsqrt(pivot)
    s = s * (1.5 - 0.5 * pivot * s * s)
    VW = jnp.concatenate([V * s, W * s], axis=1)
    S[rows, :] = VW
    high, middle, low = split(VW)
    h, m, l = (jnp.where(lane >= PAN * (g + 1), x[:, 0:BLK], 0.0) for x in (high, middle, low))
    left = jnp.concatenate([h, h, m, h, l, m], axis=0).astype(BF16)
    right = jnp.concatenate([high, middle, high, low, high, middle], axis=0).astype(BF16)
    S[...] = S[...] - mm(left, right, 0, 0, None)


def factor(A, X, S, Q, hooks):
    eye = (
        lax.broadcasted_iota(jnp.int32, (BLK, BLK), 0)
        == lax.broadcasted_iota(jnp.int32, (BLK, BLK), 1)
    ).astype(F32)
    blocks = A.shape[0] // BLK
    for k in range(blocks):
        lo, hi = BLK * k, BLK * k + BLK
        S[:, 0:BLK] = A[lo:hi, lo:hi]
        S[:, BLK : 2 * BLK] = eye

        @pl.loop(0, BLK // PAN)
        def _(g):
            panel(S, g)
            for at, hook in hooks.get(k, {}).items():
                pl.when(g == at)(hook)

        inverse = S[:, BLK : 2 * BLK]
        q = mm3(X[:, lo:hi], inverse, 1, 1)
        Q[:, lo:hi] = q.astype(BF16)
        if k < blocks - 1:
            U = mm(inverse, A[lo:hi, hi:], 1, 0)
            for at in range(hi, A.shape[0], BLK):
                u = U[:, at - hi :]
                A[at : at + BLK, at:] = A[at : at + BLK, at:] - mm(u[:, 0:BLK], u, 0, 0)
            X[:, hi:] = X[:, hi:] - mm3(q, U, 1, 0)


def scaled_update(first, second, g):
    new_first = 0.9 * first + 0.1 * g
    new_second = 0.999 * second + 0.001 * g * g
    scaled = 6.0 * (new_first / (1.0 - 0.9**10)) / (jnp.sqrt(new_second / (1.0 - 0.999**10)) + 1e-08)
    return scaled.astype(BF16)


def kernel(
    slots, bucket_of, grads, raw, first, second, delta_out, rows_out,
    X, A, S, Q, QT, G, T, RA, RB, SA, SB, XS, XR, GS, MM, MO, PB, U, GT, MT,
    loc, ds, dr, us, ur, ys, yr, tws, twr, mzs, mzr, rs, rr, xs, xr, gs, gr, es, er,
):
    dp, f = lax.axis_index("dp"), lax.axis_index("fsdp")
    z, xl, c = dp // 4, lax.rem(dp // 2, 2), lax.rem(dp, 2)
    xh, y = f // NY, lax.rem(f, NY)
    d = 1 - 2 * c

    def zat(k):
        return lax.rem(z + d * k + 2 * NZ, NZ)

    def at_z(k):
        return (zat(k) * 4 + xl * 2 + c, f)

    ahead, behind = at_z(1), at_z(-1)
    across = (z * 4 + (1 - xl) * 2 + c, f)
    twin = (z * 4 + xl * 2 + 1 - c, f)
    diagonal = (z * 4 + (1 - xl) * 2 + 1 - c, f)
    half = Q.shape[1] // 2
    columns = pl.ds(pl.multiple_of(xl * half, half), half)
    others = pl.ds(pl.multiple_of((1 - xl) * half, half), half)
    up, down = (dp, xh * NY + lax.rem(y + 1, NY)), (dp, xh * NY + lax.rem(y + NY - 1, NY))
    mirror = (z * 4 + (1 - xl) * 2 + c, (1 - xh) * NY + y)

    def remote(src, dst, send, recv, to):
        return pltpu.make_async_remote_copy(
            src_ref=src, dst_ref=dst, send_sem=send, recv_sem=recv,
            device_id=to, device_id_type=pl.DeviceIdType.MESH,
        )

    def fblock(h, yy, lo=0, n=128):
        return X.at[pl.ds(pl.multiple_of((h * NY + lax.rem(yy + 2 * NY, NY)) * 128 + lo, 64), n), :]

    def y_send(i):
        what = [
            (fblock(xh, y), up), (fblock(xh, y), down), (fblock(xh, y), mirror),
            (fblock(1 - xh, y, 64, 64), up), (fblock(1 - xh, y, 64, 64), down),
            (fblock(xh, y - 1, 0, 64), up), (fblock(xh, y + 1, 64, 64), down),
            (fblock(1 - xh, y - 1, 0, 64), up), (fblock(1 - xh, y + 1, 64, 64), down),
            (fblock(xh, y - 1, 0, 64), mirror), (fblock(xh, y + 1, 0, 64), mirror),
        ][i]
        return remote(what[0], what[0], ys.at[i], yr.at[i], what[1])

    def y_recv(i):
        what = [
            fblock(xh, y - 1), fblock(xh, y + 1), fblock(1 - xh, y),
            fblock(1 - xh, y - 1, 64, 64), fblock(1 - xh, y + 1, 64, 64),
            fblock(xh, y - 2, 0, 64), fblock(xh, y + 2, 64, 64),
            fblock(1 - xh, y - 2, 0, 64), fblock(1 - xh, y + 2, 64, 64),
            fblock(1 - xh, y - 1, 0, 64), fblock(1 - xh, y + 1, 0, 64),
        ][i]
        remote(what, what, ys.at[i], yr.at[i], up).wait_recv()

    def mblock(k):
        return MM.at[pl.ds(pl.multiple_of(zat(k) * 16, 16), 16)]

    def mz(s, way, k):
        i = s if way > 0 else 4 + s
        return remote(mblock(k), mblock(k), mzs.at[i], mzr.at[i], ahead if way > 0 else behind)

    def m_start():
        mz(0, 1, 0).start()
        mz(0, -1, 0).start()

    def m_step(s):
        mz(s - 1, 1, -s).wait_recv()
        if s < 4:
            mz(s, 1, -s).start()
            mz(s - 1, -1, s).wait_recv()
            if s < 3:
                mz(s, -1, s).start()

    pieces = (4, -3, 3, -2, 2, -1, 1, 0)

    def two_cores(k, h):
        rows = pl.ds(pl.multiple_of(zat(k) * 128 + h * 64, 64), 64)
        return G[rows, :].astype(F32) + T[rows, :].astype(F32)

    def x_piece(i):
        return remote(XS.at[i], XR.at[i], xs.at[i], xr.at[i], across)

    def x_start():
        for i, k in enumerate(pieces):
            XS[i] = two_cores(k, 1 - xl).astype(BF16)
            x_piece(i).start()

    def own(k):
        i = pieces.index(k)
        x_piece(i).wait_recv()
        return two_cores(k, xl) + XR[i].astype(F32)

    def ra(s):
        return remote(SA if s == 0 else RA.at[s - 1], RA.at[s], rs.at[s], rr.at[s], ahead)

    def rb(s):
        return remote(SB if s == 0 else RB.at[s - 1], RB.at[s], rs.at[4 + s], rr.at[4 + s], behind)

    def r_start():
        SA[...] = own(4).astype(BF16)
        ra(0).start()
        SB[...] = own(-3).astype(BF16)
        rb(0).start()

    def r_step(s):
        ra(s - 1).wait_recv()
        RA[s - 1] = (RA[s - 1].astype(F32) + own(4 - s)).astype(BF16)
        ra(s).start()
        if s < 3:
            rb(s - 1).wait_recv()
            RB[s - 1] = (RB[s - 1].astype(F32) + own(s - 3)).astype(BF16)
            rb(s).start()

    def half_sum(h):
        there = GS.at[pl.ds(pl.multiple_of(h * 64, 64), 64), :]
        return remote(there, there, xs.at[8], xr.at[8], across)

    def r_last():
        mine = own(0)
        ra(3).wait_recv()
        rb(2).wait_recv()
        GS[pl.ds(pl.multiple_of(xl * 64, 64), 64), :] = (
            mine + (RA[3].astype(F32) + RB[2].astype(F32))
        ).astype(BF16)
        half_sum(xl).start()

    def r_sum():
        half_sum(1 - xl).wait_recv()

    def pblock(k):
        return PB.at[pl.ds(pl.multiple_of(zat(k) * 8, 8), 8)]

    def gz(s, way, k):
        i = s if way > 0 else 4 + s
        return remote(pblock(k), pblock(k), gs.at[i], gr.at[i], ahead if way > 0 else behind)

    def g_start():
        part = mm(GS[...], Q[:, columns], 1, 0, None)
        pblock(0)[...] = part.reshape(8, ROWS, part.shape[1]).astype(BF16)
        gz(0, 1, 0).start()
        gz(0, -1, 0).start()

    def g_step(s):
        gz(s - 1, 1, -s).wait_recv()
        if s < 4:
            gz(s, 1, -s).start()
            gz(s - 1, -1, s).wait_recv()
            if s < 3:
                gz(s, -1, s).start()

    partners = (ahead, behind, across, twin, diagonal, up, down, mirror)
    barrier = pltpu.get_barrier_semaphore()
    for to in partners:
        pl.semaphore_signal(barrier, inc=1, device_id=to, device_id_type=pl.DeviceIdType.MESH)
    own_raw = pltpu.make_async_copy(raw.at[c], fblock(xh, y), loc.at[0])
    own_grads = pltpu.make_async_copy(grads.at[0, c], G, loc.at[1])
    own_raw.start()
    own_grads.start()
    own_moments = [
        pltpu.make_async_copy(ref, MO.at[i], loc.at[2 + i]) for i, ref in enumerate((first, second))
    ]
    for copy in own_moments:
        copy.start()
    def place(h, k):
        return MM.at[pl.ds(pl.multiple_of((z * 4 + h * 2 + k) * CAP, CAP), CAP)]

    targets = ((twin, xl, 1 - c), (across, 1 - xl, c), (diagonal, 1 - xl, 1 - c))

    def moments_to(i):
        to, h, k = targets[i]
        return remote(MT.at[i], place(xl, c), tws.at[1 + i], twr.at[1 + i], to)

    for i, copy in enumerate(own_moments):
        copy.wait()
        place(xl, c)[:, i] = MO[i, c, 0, :, :, columns].astype(BF16)
        MT[0, :, i] = MO[i, 1 - c, 0, :, :, columns].astype(BF16)
        MT[1, :, i] = MO[i, c, 0, :, :, others].astype(BF16)
        MT[2, :, i] = MO[i, 1 - c, 0, :, :, others].astype(BF16)
    own_raw.wait()
    pl.semaphore_wait(barrier, len(partners))

    for i in range(3):
        y_send(i).start()
    t_grads = remote(grads.at[0, 1 - c], T, tws.at[0], twr.at[0], twin)
    for i in range(3):
        moments_to(i).start()
    t_grads.start()
    for i, (to, h, k) in enumerate(targets):
        remote(MT.at[i], place(h, k), tws.at[1 + i], twr.at[1 + i], to).wait_recv()
    m_start()
    own_grads.wait()
    t_grads.wait_recv()
    x_start()

    def gram(yy, add):
        part = jnp.concatenate([fblock(xh, yy)[...], fblock(1 - xh, yy)[...]], axis=0)
        for lo in range(0, part.shape[1], BLK):
            product = mm(part[:, lo : lo + BLK], part[:, lo:], 0, 0)
            A[lo : lo + BLK, lo:] = A[lo : lo + BLK, lo:] + product if add else product

    for arrived, sends in ((2, (3, 4)), (0, (5, 9)), (1, (6, 10))):
        y_recv(arrived)
        for i in sends:
            y_send(i).start()
    gram(y, False)
    y_recv(4)
    y_send(8).start()
    y_recv(9)
    y_send(7).start()
    m_step(1)
    r_start()
    y_recv(3)
    gram(y - 1, True)
    y_recv(10)
    gram(y + 1, True)
    for i in range(5, 9):
        y_recv(i)
    gram(y + 2, True)
    for i in range(11):
        y_send(i).wait_send()

    hooks = {
        0: {3: lambda: r_step(1), 7: lambda: m_step(2)},
        1: {4: lambda: r_step(2)},
        2: {2: lambda: r_step(3), 5: lambda: m_step(3)},
        3: {1: r_last},
    }
    factor(A, X, S, Q, hooks)
    r_sum()
    g_start()
    m_step(4)

    for lo in range(0, Q.shape[1], BLK):
        QT[lo : lo + BLK, :] = Q[:, lo : lo + BLK].T

    def rows_of(k):
        return pl.ds(pl.multiple_of(zat(k) * 128, 128), 128)

    def u_across(i, k, part):
        there = U.at[rows_of(k), part]
        return remote(there, there, us.at[i], ur.at[i], across)

    def d_twin(i, k, at):
        there = delta_out.at[at, rows_of(k), :]
        return remote(there, there, ds.at[i], dr.at[i], twin)

    def update(i, k):
        @pl.loop(0, 8)
        def _(j):
            b = zat(k) * 8 + j
            moments = MM[slots[c, b]]
            U[pl.ds(pl.multiple_of(b * ROWS, ROWS), ROWS), columns] = scaled_update(
                moments[0].astype(F32), moments[1].astype(F32), PB[b].astype(F32)
            )

        u_across(i, k, columns).start()

    def delta(i, k):
        u_across(i, k, others).wait_recv()
        delta_out[c, rows_of(k), :] = mm(U[rows_of(k), :], QT[...], 1, 0, None).astype(BF16)
        d_twin(i, k, c).start()

    order = (0, -1, 1, -2, 2, -3, 3, 4)
    update(0, 0)
    for s in range(1, 4):
        g_step(s)
        update(2 * s - 1, -s)
        update(2 * s, s)
        for i in range(max(2 * s - 3, 0), 2 * s - 1):
            delta(i, order[i])
    g_step(4)
    update(7, 4)

    holders = ((xl, c), (xl, 1 - c), (1 - xl, c), (1 - xl, 1 - c))
    to_holders = (None, twin, across, diagonal)

    def rows_to(n, matrix, part):
        return remote(GT.at[n], rows_out.at[matrix, :, :, part], es.at[n - 1], er.at[n - 1], to_holders[n])

    for n, (h, k) in enumerate(holders):
        for i in range(CAP):
            GT[n, i] = PB[bucket_of[c, (z * 4 + h * 2 + k) * CAP + i]]
    r_own = pltpu.make_async_copy(GT.at[0], rows_out.at[c, :, :, columns], loc.at[4])
    r_own.start()
    for n in range(1, 4):
        rows_to(n, c, columns).start()
    for i in range(5, 8):
        delta(i, order[i])

    for i, k in enumerate(order):
        d_twin(i, k, c).wait_send()
        u_across(i, k, columns).wait_send()
    for i, k in enumerate(order):
        d_twin(i, -k, 1 - c).wait_recv()
    r_own.wait()
    for n in range(1, 4):
        rows_to(n, c, columns).wait_send()
    rows_to(1, 1 - c, columns).wait_recv()
    rows_to(2, c, others).wait_recv()
    rows_to(3, 1 - c, others).wait_recv()
    t_grads.wait_send()
    half_sum(xl).wait_send()
    for i in range(8):
        x_piece(i).wait_send()
    for i in range(3):
        moments_to(i).wait_send()
    for s in range(4):
        ra(s).wait_send()
        mz(s, 1, -s).wait_send()
        gz(s, 1, -s).wait_send()
    for s in range(3):
        rb(s).wait_send()
        mz(s, -1, s).wait_send()
        gz(s, -1, s).wait_send()


def shards(grads, raw_proj, bucket_owner, first_moment, second_moment):
    matrices, local_rows, features = grads.shape[1:]
    rank = raw_proj.shape[2]
    buckets = bucket_owner.shape[1]
    capacity = first_moment.shape[2]
    slot_total = lax.axis_size("dp") * capacity
    same = bucket_owner[:, :, None] == bucket_owner[:, None, :]
    index = jnp.arange(buckets)
    earlier = index[None, :] < index[:, None]
    terms = jnp.logical_and(same, earlier).astype(jnp.int32) + jnp.where(
        index[None, :] == index[:, None], capacity * bucket_owner[:, None, :], 0
    )
    slots = jnp.sum(terms, axis=-1)
    matches = slots[:, None, :] == jnp.arange(slot_total, dtype=jnp.int32)[None, :, None]
    occupied = jnp.any(matches, axis=2)
    bucket_of = jnp.sum(
        matches.astype(jnp.int32) * jnp.arange(buckets, dtype=jnp.int32)[None, None, :], axis=2
    )
    smem = pl.BlockSpec(memory_space=pltpu.SMEM)
    anywhere = pl.BlockSpec(memory_space=pl.ANY)
    piece = (local_rows // NZ // 2, features)
    dma = pltpu.SemaphoreType.DMA
    weight_delta, grad_rows = pl.pallas_call(
        kernel,
        out_shape=(
            pltpu.VMEM((matrices, local_rows, features), BF16),
            jax.ShapeDtypeStruct((matrices, capacity, ROWS, rank), BF16),
        ),
        in_specs=[smem, smem] + [anywhere] * 4,
        out_specs=(pl.BlockSpec(memory_space=pltpu.VMEM), anywhere),
        scratch_shapes=[
            pltpu.VMEM((features, rank), F32),
            pltpu.VMEM((rank, rank), F32),
            pltpu.VMEM((BLK, 2 * BLK), F32),
            pltpu.VMEM((features, rank), BF16),
            pltpu.VMEM((rank, features), BF16),
            pltpu.VMEM((local_rows, features), BF16),
            pltpu.VMEM((local_rows, features), BF16),
            pltpu.VMEM((4, *piece), BF16),
            pltpu.VMEM((3, *piece), BF16),
            pltpu.VMEM(piece, BF16),
            pltpu.VMEM(piece, BF16),
            pltpu.VMEM((8, *piece), BF16),
            pltpu.VMEM((8, *piece), BF16),
            pltpu.VMEM((local_rows // NZ, features), BF16),
            pltpu.VMEM((slot_total, 2, ROWS, rank // 2), BF16),
            pltpu.VMEM((2, *first_moment.shape), F32),
            pltpu.VMEM((buckets, ROWS, rank // 2), BF16),
            pltpu.VMEM((local_rows, rank), BF16),
            pltpu.VMEM((4, capacity, ROWS, rank // 2), BF16),
            pltpu.VMEM((3, capacity, 2, ROWS, rank // 2), BF16),
            dma((5,)), dma((8,)), dma((8,)), dma((8,)), dma((8,)),
            dma((11,)), dma((11,)), dma((4,)), dma((4,)), dma((7,)), dma((7,)),
            dma((7,)), dma((7,)), dma((9,)), dma((9,)), dma((7,)), dma((7,)), dma((3,)), dma((3,)),
        ],
        compiler_params=pltpu.CompilerParams(
            collective_id=0, has_side_effects=True, vmem_limit_bytes=56 << 20
        ),
        cost_estimate=pl.CostEstimate(
            flops=10_000_000_000, bytes_accessed=16_000_000, transcendentals=1_000_000
        ),
    )(slots, bucket_of, grads, raw_proj, first_moment, second_moment)
    start = lax.axis_index("dp") * capacity
    keep = lax.dynamic_slice_in_dim(occupied, start, capacity, 1)[:, :, None, None]
    first, second = first_moment[:, 0], second_moment[:, 0]
    grad_rows = grad_rows.astype(F32)
    first_out = jnp.where(keep, 0.9 * first + 0.1 * grad_rows, first)[:, None]
    second_out = jnp.where(keep, 0.999 * second + 0.001 * grad_rows * grad_rows, second)[:, None]
    return (weight_delta, first_out, second_out)


def solution(mesh):
    return jax.shard_map(
        shards,
        mesh=mesh,
        in_specs=(
            P("dp", None, "fsdp", None),
            P(None, "fsdp", None),
            P(None, "fsdp"),
            P(None, "fsdp", "dp", None, None),
            P(None, "fsdp", "dp", None, None),
        ),
        out_specs=(
            P(None, "fsdp", None),
            P(None, "fsdp", "dp", None, None),
            P(None, "fsdp", "dp", None, None),
        ),
        check_vma=False,
    )
```
